256 devices in a mesh: head: 4 (over z_lo), ctx: 64 (over z_hi, y, x, core).
Axes of the slice: x: 4, y: 4, z: 8 (z_hi: 2, z_lo: 4; z = z_hi * 4 + z_lo), core: 2. Of those that a mesh axis runs over, the one named last changes fastest.
Arguments:
- queries: bfloat16 [64, 256, 4096], P('ctx', 'head'), may hold values from -6 to 6
- key_state_rows: bfloat16 [64, 256, 512], P('ctx', 'head'), may hold values from -6 to 6
- value_state_rows: bfloat16 [64, 256, 512], P('ctx', 'head'), may hold values from -6 to 6
- output_state_rows: bfloat16 [64, 256, 4096], P('ctx', 'head'), may hold values from -6 to 6
- output_gradient: bfloat16 [64, 256, 4096], P('ctx', 'head'), may hold values from -0.5390625 to 0.5390625
- logsumexp_rows: float32 [64, 256, 32], P('ctx', None, 'head'), may hold values from 2 to 4
- doc_lengths: int32 [64], replicated, may hold values from 1 to 1024, 16384 in all
Outputs:
- query_grad: bfloat16 [64, 256, 4096], P('ctx', 'head')
- gradient_keys: bfloat16 [64, 256, 512], P('ctx', 'head')
- gradient_values: bfloat16 [64, 256, 512], P('ctx', 'head')
The draws below stay inside these ranges and needn't reach their ends.
Inputs may be any that keep to these rules, and one draw needn't show every extreme that they name: `doc_lengths`: the 64 lengths sum to 16384; the longest is exactly 1024.
All inputs are finite; a program needn't handle non-finite values.
Results may differ from the reference program's by a relative error of at most 0.0049.
Values may be sent and summed in bfloat16 or wider, within the bound.
A program may use at most 64 MiB of HBM per device.

```python
import math
import jax
import jax.numpy as jnp
import numpy as np
from jax import lax

QUERY_HEAD_COUNT = 32
KEY_VALUE_HEADS = 4
HEAD_WIDTH = 128
LAGS = 4
CONTEXT_TOKENS = 256
TOKENS = 16384
MAXDOC = 1024
DOCS = 64
N_CTX = 64


def shard_levels(rng, shape, shards, least, largest):
    def one(dim, parts):
        heights = jax.random.uniform(jax.random.fold_in(jax.random.fold_in(rng, 6), dim), (parts,), jnp.float32, least / len(shards), largest / len(shards))
        return jnp.repeat(jnp.exp(heights), shape[dim] // parts).reshape((-1,) + (1,) * (len(shape) - dim - 1))

    gain = one(*shards[0])
    for cut in shards[1:]:
        gain = gain * one(*cut)
    return gain


def length_profile(number_of, total, bound, skew):
    weights = [(1 << 20) // math.isqrt(standing ** skew) + 1 for standing in range(2, number_of + 1)]
    spare, holding = total - bound - (number_of - 1), [1] * (number_of - 1)
    while spare > 0:
        movable = [i for i in range(number_of - 1) if holding[i] < bound]
        whole, budget = sum([weights[i] for i in movable]), spare
        for i in movable:
            addition = min(bound - holding[i], max(1, budget * weights[i] // whole), spare)
            holding[i] = holding[i] + addition
            spare = spare - addition
    return np.array([bound] + holding)


def uneven_parts(key, number_of, total, reach, lean):
    if number_of == 2:
        one = jax.random.randint(key, (), max(1, total - reach), min(reach, total - 1) + 1)
        return jnp.stack([one, total - one])
    lengths = jnp.asarray(length_profile(number_of, total, reach, lean), jnp.int32)
    couples = (number_of - 1) // 2
    giver, receiver = lengths[1:1 + 2 * couples:2], lengths[2:2 + 2 * couples:2]
    room = jnp.minimum(giver - 1, reach - receiver)
    passed = jax.random.randint(jax.random.fold_in(key, 1), (couples,), 0, 1 << 20) % (room + 1)
    lengths = lengths.at[1:1 + 2 * couples:2].set(giver - passed).at[2:2 + 2 * couples:2].set(receiver + passed)
    return lengths[jax.random.permutation(jax.random.fold_in(key, 2), number_of)]


def centred(own_key, extent, scale, bound, cuts=(), held_as=jnp.bfloat16):
    entries = jax.random.normal(own_key, extent, jnp.float32) * scale
    if len(cuts) > 0:
        entries = shard_levels(own_key, extent, cuts, -0.22, 0.18) * entries
    return jnp.clip(entries, min=-bound, max=bound).astype(held_as)


def setup_inputs(seed: int = 0) -> dict:
    seeds = jax.random.split(jax.random.key(seed), 8)
    return {
        "queries": centred(seeds[0], (N_CTX, CONTEXT_TOKENS, QUERY_HEAD_COUNT * HEAD_WIDTH), 1.0, 6.0, ((0, 64), (1, 4))),
        "key_state_rows": centred(seeds[1], (N_CTX, CONTEXT_TOKENS, KEY_VALUE_HEADS * HEAD_WIDTH), 1.0, 6.0, ((0, 64), (1, 4))),
        "value_state_rows": centred(seeds[2], (N_CTX, CONTEXT_TOKENS, KEY_VALUE_HEADS * HEAD_WIDTH), 1.0, 6.0, ((0, 64), (1, 4))),
        "output_state_rows": centred(seeds[3], (N_CTX, CONTEXT_TOKENS, QUERY_HEAD_COUNT * HEAD_WIDTH), 1.0, 6.0, ((0, 64), (1, 4))),
        "output_gradient": centred(seeds[4], (N_CTX, CONTEXT_TOKENS, QUERY_HEAD_COUNT * HEAD_WIDTH), 0.09, 0.5390625, ((0, 64), (1, 4))),
        "logsumexp_rows": jnp.clip(2.0 + 2.0 * jax.random.uniform(seeds[5], (N_CTX, CONTEXT_TOKENS, QUERY_HEAD_COUNT), jnp.float32) ** shard_levels(seeds[5], (N_CTX, CONTEXT_TOKENS, QUERY_HEAD_COUNT), ((0, 64), (2, 4)), -0.2, 0.2), 2.0, 4.0),
        "doc_lengths": uneven_parts(seeds[6], DOCS, TOKENS, MAXDOC, 2).astype(jnp.int32),
    }


def segment_of(positions, starts):
    return jnp.sum((starts[None, :] <= positions[:, None]).astype(jnp.int32), axis=1) - 1


def block_terms(query_block, grad_block, sums_turned, delta_turned, key_block, value_block, allowed):
    score_scale = HEAD_WIDTH ** -0.5
    query_wide = query_block.astype(jnp.float32)
    grad_wide = grad_block.astype(jnp.float32)
    key_wide = key_block.astype(jnp.float32)
    value_wide = value_block.astype(jnp.float32)
    scores = jnp.einsum("ikgd,jkd->kgij", query_wide, key_wide) * score_scale
    weights = jnp.where(allowed[None, None], jnp.exp(scores - sums_turned), 0.0)
    grad_scores = jnp.einsum("ikgd,jkd->kgij", grad_wide, value_wide)
    shifted = (weights * (grad_scores - delta_turned) * score_scale).astype(jnp.bfloat16)
    rounded = weights.astype(jnp.bfloat16)
    value_part = jnp.einsum("kgij,ikgd->jkd", rounded.astype(jnp.float32), grad_wide)
    key_part = jnp.einsum("kgij,ikgd->jkd", shifted.astype(jnp.float32), query_wide)
    query_part = jnp.einsum("kgij,jkd->ikgd", shifted.astype(jnp.float32), key_wide)
    return query_part, key_part, value_part


def reference(queries, key_state_rows, value_state_rows, output_state_rows, output_gradient, logsumexp_rows, doc_lengths):
    block_list = N_CTX
    row_list = CONTEXT_TOKENS
    group_count = QUERY_HEAD_COUNT // KEY_VALUE_HEADS
    starts = (jnp.cumsum(doc_lengths) - doc_lengths).astype(jnp.int32)
    query_every = queries.reshape(block_list, row_list, KEY_VALUE_HEADS, group_count, HEAD_WIDTH)
    gradient_every = output_gradient.reshape(block_list, row_list, KEY_VALUE_HEADS, group_count, HEAD_WIDTH)
    output_every = output_state_rows.reshape(block_list, row_list, KEY_VALUE_HEADS, group_count, HEAD_WIDTH)
    key_every = key_state_rows.reshape(block_list, row_list, KEY_VALUE_HEADS, HEAD_WIDTH)
    value_every = value_state_rows.reshape(block_list, row_list, KEY_VALUE_HEADS, HEAD_WIDTH)
    delta_all = jnp.sum(gradient_every.astype(jnp.float32) * output_every.astype(jnp.float32), axis=-1)
    sum_every = logsumexp_rows.reshape(block_list, row_list, KEY_VALUE_HEADS, group_count)
    offsets = jnp.arange(row_list, dtype=jnp.int32)
    blank_terms = (jnp.zeros((row_list, KEY_VALUE_HEADS, group_count, HEAD_WIDTH), jnp.float32),
                   jnp.zeros((row_list, KEY_VALUE_HEADS, HEAD_WIDTH), jnp.float32),
                   jnp.zeros((row_list, KEY_VALUE_HEADS, HEAD_WIDTH), jnp.float32))

    def step(carry, block_index):
        key_gradient_list, value_gradient_list = carry
        query_pos = block_index * row_list + offsets
        query_seg = segment_of(query_pos, starts)
        query_block = query_every[block_index]
        grad_block = gradient_every[block_index]
        sums_turned = jnp.transpose(sum_every[block_index], (1, 2, 0))[..., None]
        delta_turned = jnp.transpose(delta_all[block_index], (1, 2, 0))[..., None]
        query_overall = jnp.zeros((row_list, KEY_VALUE_HEADS, group_count, HEAD_WIDTH), jnp.float32)
        for distance in range(LAGS + 1):
            source = jnp.maximum(block_index - distance, 0).astype(jnp.int32)
            key_pos = (block_index - distance) * row_list + offsets
            key_seg = segment_of(key_pos, starts)
            allowed = ((query_seg[:, None] == key_seg[None, :])
                       & (key_pos[None, :] <= query_pos[:, None])
                       & (key_pos[None, :] >= 0))
            key_block = key_every[source]
            value_block = value_every[source]
            query_part, key_part, value_part = lax.cond(
                jnp.any(allowed),
                lambda: block_terms(query_block, grad_block, sums_turned, delta_turned,
                                    key_block, value_block, allowed),
                lambda: blank_terms)
            query_overall = query_overall + query_part
            key_gradient_list = key_gradient_list.at[source].add(key_part)
            value_gradient_list = value_gradient_list.at[source].add(value_part)
        return (key_gradient_list, value_gradient_list), query_overall

    initial_carry = (jnp.zeros((block_list, row_list, KEY_VALUE_HEADS, HEAD_WIDTH), jnp.float32),
                   jnp.zeros((block_list, row_list, KEY_VALUE_HEADS, HEAD_WIDTH), jnp.float32))
    (key_gradient_list, value_gradient_list), query_grads = lax.scan(step, initial_carry, jnp.arange(block_list, dtype=jnp.int32))
    query_grad = query_grads.reshape(block_list, row_list, QUERY_HEAD_COUNT * HEAD_WIDTH).astype(jnp.bfloat16)
    gradient_keys = key_gradient_list.reshape(block_list, row_list, KEY_VALUE_HEADS * HEAD_WIDTH).astype(jnp.bfloat16)
    gradient_values = value_gradient_list.reshape(block_list, row_list, KEY_VALUE_HEADS * HEAD_WIDTH).astype(jnp.bfloat16)
    return query_grad, gradient_keys, gradient_values
```

```python
import jax
import jax.numpy as jnp
from jax import lax
from jax.experimental import pallas as pl
from jax.experimental.pallas import tpu as pltpu
from jax.sharding import PartitionSpec as P

MESH = pl.DeviceIdType.MESH
F32 = jnp.float32
BF16 = jnp.bfloat16
SCALE = 128 ** (-0.5)
GROUPS = 16


def kernel(
    q_ref, k_ref, v_ref, o_ref, do_ref, lse_ref, len_ref,
    dq_ref, dk_ref, dv_ref,
    kvs, kvb, qb, dob, lsec, lset, lseb, dls, dlb, acc, dqt, dqs, dqr, pxs, pxr, rts, ret,
    s_kv, s_kvn, r_kv, s_kvp, r_kvp, s_q, r_q, s_do, r_do,
    s_l, r_l, s_d, r_d, s_dq, r_dq, s_px, r_px, s_rt, s_rtp, r_rt, r_rtn,
):
    z = lax.axis_index("head")
    c = lax.axis_index("ctx")
    pair = c // 4
    own = c % 4
    xq = own // 2
    core = c % 2
    zb = z % 2
    zp = z // 2
    g = 2 * xq + zb
    first = pair == 0
    last = pair == GROUPS - 1

    def zx(e):
        return (z, z + 1 - 2 * zb, (z + 2) % 4, 3 - z)[e]

    def xx(a):
        return xq if a == 0 else 1 - xq

    def kx(b):
        return core if b == 0 else 1 - core

    def at(off, a, b):
        return 4 * (pair + off) + 2 * xx(a) + kx(b)

    def remote(src, dst, ssem, rsem, dev):
        return pltpu.make_async_remote_copy(
            src_ref=src, dst_ref=dst, send_sem=ssem, recv_sem=rsem,
            device_id=dev, device_id_type=MESH,
        )

    def await_bytes(ref, sem):
        pltpu.make_async_copy(ref, ref, sem).wait()

    barrier = pltpu.get_barrier_semaphore()
    for a in range(2):
        for b in range(2):
            for e in range(4):
                if a or b or e:
                    pl.semaphore_signal(barrier, inc=1, device_id=(zx(e), at(0, a, b)), device_id_type=MESH)

    @pl.when(jnp.logical_not(first))
    def _():
        for a in range(2):
            for e in range(4):
                pl.semaphore_signal(barrier, inc=1, device_id=(zx(e), at(-1, a, 0)), device_id_type=MESH)

    @pl.when(jnp.logical_not(last))
    def _():
        for a in range(2):
            for e in range(4):
                pl.semaphore_signal(barrier, inc=1, device_id=(zx(e), at(1, a, 0)), device_id_type=MESH)

    for n in range(4):
        kvs[:, n * 256 : n * 256 + 128] = k_ref[0, :, n * 128 : (n + 1) * 128]
        kvs[:, n * 256 + 128 : (n + 1) * 256] = v_ref[0, :, n * 128 : (n + 1) * 128]

    pl.semaphore_wait(barrier, 15 + 8 * ((pair + GROUPS - 1) // GROUPS) + 8 * ((2 * GROUPS - 2 - pair) // GROUPS))

    def send_kv(off):
        slot = 4 * (1 - off) + own
        for a in range(2):
            for e in range(4):
                there = 2 * xx(a) + zx(e) % 2
                src = kvs.at[:, pl.ds(pl.multiple_of(there * 256, 256), 256)]
                dst = kvb.at[pl.ds(pl.multiple_of(slot * 256 + z * 64, 64), 64)]
                if off == 0 and a == 0 and e == 0:
                    pltpu.make_async_copy(src, dst, r_kv.at[slot]).start()
                else:
                    remote(src, dst, s_kvn if off else s_kv, r_kv.at[slot], (zx(e), at(off, a, 0))).start()

    send_kv(0)

    @pl.when(jnp.logical_not(last))
    def _():
        send_kv(1)

    rows_own = pl.ds(pl.multiple_of(own * 128 + zb * 64, 64), 64)
    for a in range(2):
        for b in range(2):
            for e in range(2):
                lane = (2 * xx(a) + zx(e) % 2) * 1024 + kx(b) * 512
                cols = pl.ds(pl.multiple_of(lane, 512), 512)
                for ref, buf, ss, rr in ((q_ref, qb, s_q, r_q), (do_ref, dob, s_do, r_do)):
                    src = ref.at[0, :, cols]
                    dst = buf.at[rows_own]
                    if a or b or e:
                        remote(src, dst, ss, rr.at[own], (zx(e), at(0, a, b))).start()
                    else:
                        pltpu.make_async_copy(src, dst, rr.at[own]).start()

    lsec[...] = jnp.zeros_like(lsec)
    lsec[:, 0:8] = lse_ref[0]
    turned = lsec[...].T
    for p in range(2):
        lset[p] = turned[0:8, p * 128 : (p + 1) * 128]
    to_x = z // 2
    for e in (0, 2):
        half = zx(e) // 2
        for b in range(2):
            dev = (zx(e), 4 * pair + 2 * to_x + kx(b))
            src, dst = lset.at[half], lseb.at[own]
            if e == 0 and b == 0:
                @pl.when(to_x == xq)
                def _():
                    pltpu.make_async_copy(src, dst, r_l.at[own]).start()

                @pl.when(to_x != xq)
                def _():
                    remote(src, dst, s_l.at[0], r_l.at[own], dev).start()
            else:
                remote(src, dst, s_l.at[e + b], r_l.at[own], dev).start()

    lanes = lax.broadcasted_iota(jnp.int32, (64, 128), 1)
    delta = jnp.zeros((64, 128), F32)
    for n in range(32):
        part = do_ref[0, :, n * 128 : (n + 1) * 128].astype(F32) * o_ref[0, :, n * 128 : (n + 1) * 128].astype(F32)
        delta = jnp.where(lanes == n, jnp.sum(part, axis=1, keepdims=True), delta)
    both = jnp.concatenate([delta, delta], axis=0).T
    for n in range(4):
        dls[n] = both[n * 8 : (n + 1) * 8]
    for a in range(2):
        for b in range(2):
            for e in range(2):
                src = dls.at[2 * xx(a) + zx(e) % 2]
                dst = dlb.at[pl.ds(pl.multiple_of(own * 16 + zb * 8, 8), 8)]
                if a or b or e:
                    remote(src, dst, s_d, r_d.at[own], (zx(e), at(0, a, b))).start()
                else:
                    pltpu.make_async_copy(src, dst, r_d.at[own]).start()

    place = lax.broadcasted_iota(jnp.int32, (8, 128), 1) + (pair * 1024 + zp * 128)

    def seek(d, carry):
        begin, found = carry
        found = tuple(jnp.where(place + 256 * n >= begin, begin, f) for n, f in enumerate(found))
        return begin + len_ref[d], found

    _, opens = lax.fori_loop(0, 64, seek, (jnp.int32(0), tuple(jnp.zeros((8, 128), jnp.int32) for _ in range(4))))
    for n in range(4):
        dqt[n] = jnp.zeros((128, 512), F32)
    acc[...] = jnp.zeros_like(acc)

    @pl.when(first)
    def _():
        kvb[0:1024] = jnp.zeros((1024, 256), BF16)

    def blk(b):
        return pl.ds(pl.multiple_of(b * 256, 256), 256)

    partner = (z, at(0, 0, 1))
    for i in range(4):
        b = 2 * i + core

        def hand_on():
            await_bytes(kvb.at[blk(b)], r_kv.at[b])
            remote(kvb.at[blk(b)], kvb.at[blk(b)], s_kvp, r_kvp.at[b], partner).start()

        if i < 2:
            pl.when(jnp.logical_not(first))(hand_on)
        else:
            hand_on()
    for i in range(4):
        b = 2 * i + 1 - core

        def take():
            await_bytes(kvb.at[blk(b)], r_kvp.at[b])

        if i < 2:
            pl.when(jnp.logical_not(first))(take)
        else:
            take()

    for n in range(4):
        await_bytes(lseb.at[n], r_l.at[n])
        await_bytes(dlb.at[n * 16 : n * 16 + 16], r_d.at[n])
        await_bytes(qb.at[n * 128 : n * 128 + 128], r_q.at[n])
        await_bytes(dob.at[n * 128 : n * 128 + 128], r_do.at[n])
    steps = lax.broadcasted_iota(jnp.int32, (256, 128), 0)
    low = lax.broadcasted_iota(jnp.int32, (8, 128), 1) < 64

    def piece(j):
        bx = (xq + j // 2) % 2
        bk = (core + j % 2) % 2
        bi = 2 * bx + bk
        mine = pl.ds(pl.multiple_of(bi * 128, 128), 128)
        deltas = dlb.at[pl.ds(pl.multiple_of(bi * 16, 16), 16)]
        lse_all = lseb[bi]
        delta_all = jnp.where(low, deltas[0:8], deltas[8:16])
        lse_mine = jnp.where(core == 0, lse_all[0:4], lse_all[4:8])
        delta_mine = jnp.where(core == 0, delta_all[0:4], delta_all[4:8])
        lse_row = jnp.concatenate([lse_mine[n : n + 1] for n in range(4)], axis=1)
        delta_row = jnp.concatenate([delta_mine[n : n + 1] for n in range(4)], axis=1)
        where_open = jnp.where(bi == 0, opens[0], jnp.where(bi == 1, opens[1], jnp.where(bi == 2, opens[2], opens[3])))[0:1]
        where_here = (place + 256 * bi)[0:1]
        qp = qb[mine]
        dop = dob[mine]
        qm = jnp.concatenate([qp[:, n * 128 : (n + 1) * 128] for n in range(4)], axis=0)
        dom = jnp.concatenate([dop[:, n * 128 : (n + 1) * 128] for n in range(4)], axis=0)

        def lag(l, _):
            b = bi + l
            rows = blk(b)
            key = kvb[rows, 0:128]
            value = kvb[rows, 128:256]
            base = (4 * pair - 4 + b) * 256
            allowed = (steps >= where_open - base) & (steps <= where_here - base)
            allowed = jnp.concatenate([allowed] * 4, axis=1)
            scores = lax.dot_general(key, qm, (((1,), (1,)), ((), ())), preferred_element_type=F32)
            weights = jnp.where(allowed, jnp.exp(scores * SCALE - lse_row), 0.0)
            grads = lax.dot_general(value, dom, (((1,), (1,)), ((), ())), preferred_element_type=F32)
            shifted = (weights * (grads - delta_row) * SCALE).astype(BF16)
            acc[rows, 128:256] += jnp.dot(weights.astype(BF16), dom, preferred_element_type=F32)
            acc[rows, 0:128] += jnp.dot(shifted, qm, preferred_element_type=F32)
            dqt[bi] += lax.dot_general(key, shifted, (((0,), (0,)), ((), ())), preferred_element_type=F32)
            return 0

        lax.fori_loop(0, 5, lag, 0)
        done = dqt[bi]
        for n in range(4):
            dqs[j * 128 : (j + 1) * 128, n * 128 : (n + 1) * 128] = done[:, n * 128 : (n + 1) * 128].T.astype(BF16)
    slot = 2 * g + core
    for j in range(4):
        piece(j)
    for j in range(4):
        bx = (xq + j // 2) % 2
        bk = (core + j % 2) % 2
        bi = 2 * bx + bk
        for e in range(2):
            src = dqs.at[pl.ds(pl.multiple_of(j * 128 + (zx(e) % 2) * 64, 64), 64)]
            dst = dqr.at[slot]
            if e:
                remote(src, dst, s_dq, r_dq, (zx(1), 4 * pair + bi)).start()
            elif j:
                remote(src, dst, s_dq, r_dq, (z, 4 * pair + bi)).start()
            else:
                pltpu.make_async_copy(src, dst, r_dq).start()

    for i in range(4):
        pxs[i] = acc[blk(2 * i + 1 - core)].astype(BF16)
        remote(pxs.at[i], pxr.at[i], s_px, r_px.at[i], partner).start()

    def send_back(off):
        for a in range(2):
            i = (2 * (1 - off)) + xx(a)
            for e in range(4):
                src = rts.at[i, pl.ds(pl.multiple_of(zx(e) * 64, 64), 64)]
                dst = ret.at[off * 8 + z * 2 + xq]
                if off == 0 and a == 0 and e == 0:
                    pltpu.make_async_copy(src, dst, r_rt).start()
                else:
                    remote(src, dst, s_rtp if off else s_rt, r_rtn if off else r_rt, (zx(e), at(-off, a, 0))).start()

    for i in range(2):
        await_bytes(pxr.at[i], r_px.at[i])
        rts[i] = (acc[blk(2 * i + core)] + pxr[i].astype(F32)).astype(BF16)

    @pl.when(jnp.logical_not(first))
    def _():
        send_back(1)

    for i in range(2, 4):
        await_bytes(pxr.at[i], r_px.at[i])
        rts[i] = (acc[blk(2 * i + core)] + pxr[i].astype(F32)).astype(BF16)
    send_back(0)

    await_bytes(ret.at[0:8], r_rt)

    @pl.when(last)
    def _():
        ret[8:16] = jnp.zeros((8, 64, 256), BF16)

    @pl.when(jnp.logical_not(last))
    def _():
        await_bytes(ret.at[8:16], r_rtn)

    for n in range(4):
        total = jnp.zeros((64, 256), F32)
        for off in range(2):
            for p in range(2):
                total = total + ret[off * 8 + (2 * p + n % 2) * 2 + n // 2].astype(F32)
        dk_ref[0, :, n * 128 : (n + 1) * 128] = total[:, 0:128].astype(BF16)
        dv_ref[0, :, n * 128 : (n + 1) * 128] = total[:, 128:256].astype(BF16)

    await_bytes(dqr, r_dq)
    for n in range(8):
        dq_ref[0, :, n * 512 : (n + 1) * 512] = dqr[n]

    await_bytes(kvb.at[0 : 7 * 64], s_kv)
    await_bytes(qb.at[0 : 7 * 64], s_q)
    await_bytes(dob.at[0 : 7 * 64], s_do)
    await_bytes(dqs.at[0 : 7 * 64], s_dq)
    await_bytes(pxs, s_px)
    await_bytes(ret.at[0:7], s_rt)
    await_bytes(dlb.at[0 : 7 * 8], s_d)
    for n in range(1, 4):
        await_bytes(lset.at[0], s_l.at[n])

    @pl.when(to_x != xq)
    def _():
        await_bytes(lset.at[0], s_l.at[0])

    @pl.when(jnp.logical_not(last))
    def _():
        await_bytes(kvb.at[0:512], s_kvn)

    @pl.when(first)
    def _():
        await_bytes(kvb.at[0:512], s_kvp)

    @pl.when(jnp.logical_not(first))
    def _():
        await_bytes(kvb.at[0:1024], s_kvp)
        await_bytes(ret.at[0:8], s_rtp)


def local(queries, keys, values, outputs, gradient, sums, lengths):
    vmem = pl.BlockSpec(memory_space=pltpu.VMEM)
    dma = pltpu.SemaphoreType.DMA
    return pl.pallas_call(
        kernel,
        out_shape=(
            jax.ShapeDtypeStruct((1, 64, 4096), BF16),
            jax.ShapeDtypeStruct((1, 64, 512), BF16),
            jax.ShapeDtypeStruct((1, 64, 512), BF16),
        ),
        in_specs=[vmem] * 6 + [pl.BlockSpec(memory_space=pltpu.SMEM)],
        out_specs=(vmem, vmem, vmem),
        scratch_shapes=[
            pltpu.VMEM((64, 1024), BF16),
            pltpu.VMEM((2048, 256), BF16),
            pltpu.VMEM((512, 512), BF16),
            pltpu.VMEM((512, 512), BF16),
            pltpu.VMEM((256, 128), F32),
            pltpu.VMEM((2, 8, 128), F32),
            pltpu.VMEM((4, 8, 128), F32),
            pltpu.VMEM((4, 8, 128), F32),
            pltpu.VMEM((64, 128), F32),
            pltpu.VMEM((2048, 256), F32),
            pltpu.VMEM((4, 128, 512), F32),
            pltpu.VMEM((512, 512), BF16),
            pltpu.VMEM((8, 64, 512), BF16),
            pltpu.VMEM((4, 256, 256), BF16),
            pltpu.VMEM((4, 256, 256), BF16),
            pltpu.VMEM((4, 256, 256), BF16),
            pltpu.VMEM((16, 64, 256), BF16),
            dma, dma, dma((8,)), dma, dma((8,)), dma, dma((4,)), dma, dma((4,)),
            dma((4,)), dma((4,)), dma, dma((4,)), dma, dma, dma, dma((4,)), dma, dma, dma, dma,
        ],
        compiler_params=pltpu.CompilerParams(
            collective_id=0, has_side_effects=True, vmem_limit_bytes=48 * 2**20
        ),
        name="attention_backward",
    )(queries, keys, values, outputs, gradient, sums, lengths)


def solution(mesh):
    in_specs = (
        P("ctx", "head", None),
        P("ctx", "head", None),
        P("ctx", "head", None),
        P("ctx", "head", None),
        P("ctx", "head", None),
        P("ctx", None, "head"),
        P(),
    )
    out_specs = (P("ctx", "head", None), P("ctx", "head", None), P("ctx", "head", None))
    return jax.shard_map(local, mesh=mesh, in_specs=in_specs, out_specs=out_specs, check_vma=False)
```

```python
import jax
import jax.numpy as jnp
from jax import lax
from jax.experimental import pallas as pl
from jax.experimental.pallas import tpu as pltpu
from jax.sharding import PartitionSpec as P

MESH = pl.DeviceIdType.MESH
F32 = jnp.float32
BF16 = jnp.bfloat16
SCALE = 128 ** (-0.5)
GROUPS = 16


def kernel(
    q_ref, k_ref, v_ref, o_ref, do_ref, lse_ref, len_ref,
    dq_ref, dk_ref, dv_ref,
    kin, ov, dov, kvs, kvb, qb, dob, lset, lseb, dls, dlb, acc, dqt, dqs, dqr, pxs, pxr, rts, ret,
    s_in, s_kv, s_kvn, r_kv, s_kvp, r_kvp, s_q, r_q, s_do, r_do,
    s_l, r_l, s_d, r_d, s_dq, r_dq, s_px, r_px, s_rt, s_rtp, r_rt, r_rtn,
):
    z = lax.axis_index("head")
    c = lax.axis_index("ctx")
    pair = c // 4
    own = c % 4
    xq = own // 2
    core = c % 2
    zb = z % 2
    zp = z // 2
    g = 2 * xq + zb
    first = pair == 0
    last = pair == GROUPS - 1

    def zx(e):
        return (z, z + 1 - 2 * zb, (z + 2) % 4, 3 - z)[e]

    def xx(a):
        return xq if a == 0 else 1 - xq

    def kx(b):
        return core if b == 0 else 1 - core

    def at(off, a, b):
        return 4 * (pair + off) + 2 * xx(a) + kx(b)

    def remote(src, dst, ssem, rsem, dev):
        return pltpu.make_async_remote_copy(
            src_ref=src, dst_ref=dst, send_sem=ssem, recv_sem=rsem,
            device_id=dev, device_id_type=MESH,
        )

    def await_bytes(ref, sem):
        pltpu.make_async_copy(ref, ref, sem).wait()

    barrier = pltpu.get_barrier_semaphore()
    for a in range(2):
        for b in range(2):
            for e in range(4):
                if a or b or e:
                    pl.semaphore_signal(barrier, inc=1, device_id=(zx(e), at(0, a, b)), device_id_type=MESH)

    @pl.when(jnp.logical_not(first))
    def _():
        for a in range(2):
            for e in range(4):
                pl.semaphore_signal(barrier, inc=1, device_id=(zx(e), at(-1, a, 0)), device_id_type=MESH)

    @pl.when(jnp.logical_not(last))
    def _():
        for a in range(2):
            for e in range(4):
                pl.semaphore_signal(barrier, inc=1, device_id=(zx(e), at(1, a, 0)), device_id_type=MESH)

    loads = [
        pltpu.make_async_copy(src, dst, s_in.at[n])
        for n, (src, dst) in enumerate(
            ((k_ref.at[0], kin.at[0]), (v_ref.at[0], kin.at[1]), (lse_ref.at[0], lset), (do_ref.at[0], dov), (o_ref.at[0], ov))
        )
    ]
    for load in loads:
        load.start()
    acc[...] = jnp.zeros_like(acc)

    place = lax.broadcasted_iota(jnp.int32, (8, 128), 1) + (pair * 1024 + zp * 128)

    def block_of(j):
        return 2 * ((xq + j // 2) % 2) + (core + j % 2) % 2

    def seek(d, carry):
        begin, found = carry
        found = tuple(jnp.where(place + 256 * block_of(n) >= begin, begin, f) for n, f in enumerate(found))
        return begin + len_ref[d], found

    _, opens = lax.fori_loop(0, 64, seek, (jnp.int32(0), tuple(jnp.zeros((8, 128), jnp.int32) for _ in range(4))))

    for load in loads[:2]:
        load.wait()
    for n in range(4):
        kvs[:, n * 256 : n * 256 + 128] = kin[0, :, n * 128 : (n + 1) * 128]
        kvs[:, n * 256 + 128 : (n + 1) * 256] = kin[1, :, n * 128 : (n + 1) * 128]

    for load in loads[2:]:
        load.wait()
    lanes = lax.broadcasted_iota(jnp.int32, (64, 128), 1)
    delta = jnp.zeros((64, 128), F32)
    for n in range(32):
        part = dov[:, n * 128 : (n + 1) * 128].astype(F32) * ov[:, n * 128 : (n + 1) * 128].astype(F32)
        delta = jnp.where(lanes == n, jnp.sum(part, axis=1, keepdims=True), delta)
    both = jnp.concatenate([delta, delta], axis=0).T
    for n in range(4):
        dls[n] = both[n * 8 : (n + 1) * 8]

    pl.semaphore_wait(barrier, 15 + 8 * ((pair + GROUPS - 1) // GROUPS) + 8 * ((2 * GROUPS - 2 - pair) // GROUPS))

    def send_kv(off):
        slot = 4 * (1 - off) + own
        for a in range(2):
            for e in range(4):
                there = 2 * xx(a) + zx(e) % 2
                src = kvs.at[:, pl.ds(pl.multiple_of(there * 256, 256), 256)]
                dst = kvb.at[pl.ds(pl.multiple_of(slot * 256 + z * 64, 64), 64)]
                if off == 0 and a == 0 and e == 0:
                    pltpu.make_async_copy(src, dst, r_kv.at[slot]).start()
                else:
                    remote(src, dst, s_kvn if off else s_kv, r_kv.at[slot], (zx(e), at(off, a, 0))).start()

    send_kv(0)

    @pl.when(jnp.logical_not(last))
    def _():
        send_kv(1)

    for a in range(2):
        for b in range(2):
            for e in range(2):
                lane = (2 * xx(a) + zx(e) % 2) * 1024 + kx(b) * 512
                cols = pl.ds(pl.multiple_of(lane, 512), 512)
                for ref, buf, ss, rr in ((q_ref, qb, s_q, r_q), (do_ref, dob, s_do, r_do)):
                    src = ref.at[0, :, cols]
                    slot = 2 * a + b
                    dst = buf.at[pl.ds(pl.multiple_of(slot * 128 + zb * 64, 64), 64)]
                    if a or b or e:
                        remote(src, dst, ss, rr.at[slot], (zx(e), at(0, a, b))).start()
                    else:
                        pltpu.make_async_copy(src, dst, rr.at[slot]).start()

    to_x = z // 2
    for e in (0, 2):
        half = zx(e) // 2
        for b in range(2):
            dev = (zx(e), 4 * pair + 2 * to_x + kx(b))
            slot = 2 * ((to_x + xq) % 2) + b
            src, dst = lset.at[:, pl.ds(pl.multiple_of(half * 128, 128), 128)], lseb.at[slot]
            if e == 0 and b == 0:
                @pl.when(to_x == xq)
                def _():
                    pltpu.make_async_copy(src, dst, r_l.at[slot]).start()

                @pl.when(to_x != xq)
                def _():
                    remote(src, dst, s_l.at[0], r_l.at[slot], dev).start()
            else:
                remote(src, dst, s_l.at[e + b], r_l.at[slot], dev).start()

    for a in range(2):
        for b in range(2):
            for e in range(2):
                src = dls.at[2 * xx(a) + zx(e) % 2]
                slot = 2 * a + b
                dst = dlb.at[pl.ds(pl.multiple_of(slot * 16 + zb * 8, 8), 8)]
                if a or b or e:
                    remote(src, dst, s_d, r_d.at[slot], (zx(e), at(0, a, b))).start()
                else:
                    pltpu.make_async_copy(src, dst, r_d.at[slot]).start()

    for n in range(4):
        dqt[n] = jnp.zeros((128, 512), F32)
    @pl.when(first)
    def _():
        kvb[0:1024] = jnp.zeros((1024, 256), BF16)

    def blk(b):
        return pl.ds(pl.multiple_of(b * 256, 256), 256)

    partner = (z, at(0, 0, 1))
    for i in range(4):
        b = 2 * i + core

        def hand_on():
            await_bytes(kvb.at[blk(b)], r_kv.at[b])
            remote(kvb.at[blk(b)], kvb.at[blk(b)], s_kvp, r_kvp.at[b], partner).start()

        if i < 2:
            pl.when(jnp.logical_not(first))(hand_on)
        else:
            hand_on()
    for i in range(4):
        b = 2 * i + 1 - core

        def take():
            await_bytes(kvb.at[blk(b)], r_kvp.at[b])

        if i < 2:
            pl.when(jnp.logical_not(first))(take)
        else:
            take()

    steps = lax.broadcasted_iota(jnp.int32, (256, 128), 0)
    low = lax.broadcasted_iota(jnp.int32, (8, 128), 1) < 64

    def work(j, begin, end):
        bi = block_of(j)
        lse_all = lseb[j]
        delta_all = jnp.where(low, dlb[j * 16 : j * 16 + 8], dlb[j * 16 + 8 : j * 16 + 16])
        lse_mine = jnp.where(core == 0, lse_all[0:4], lse_all[4:8])
        delta_mine = jnp.where(core == 0, delta_all[0:4], delta_all[4:8])
        lse_row = jnp.concatenate([lse_mine[n : n + 1] for n in range(4)], axis=1)
        delta_row = jnp.concatenate([delta_mine[n : n + 1] for n in range(4)], axis=1)
        where_open = opens[j][0:1]
        where_here = (place + 256 * bi)[0:1]
        qp = qb[j * 128 : (j + 1) * 128]
        dop = dob[j * 128 : (j + 1) * 128]
        qm = jnp.concatenate([qp[:, n * 128 : (n + 1) * 128] for n in range(4)], axis=0)
        dom = jnp.concatenate([dop[:, n * 128 : (n + 1) * 128] for n in range(4)], axis=0)

        def lag(b, _):
            rows = blk(b)
            key = kvb[rows, 0:128]
            value = kvb[rows, 128:256]
            base = (4 * pair - 4 + b) * 256
            allowed = (steps >= where_open - base) & (steps <= where_here - base)
            allowed = jnp.concatenate([allowed] * 4, axis=1)
            scores = lax.dot_general(key, qm, (((1,), (1,)), ((), ())), preferred_element_type=F32)
            weights = jnp.where(allowed, jnp.exp(scores * SCALE - lse_row), 0.0)
            grads = lax.dot_general(value, dom, (((1,), (1,)), ((), ())), preferred_element_type=F32)
            shifted = (weights * (grads - delta_row) * SCALE).astype(BF16)
            acc[rows, 128:256] += jnp.dot(weights.astype(BF16), dom, preferred_element_type=F32)
            acc[rows, 0:128] += jnp.dot(shifted, qm, preferred_element_type=F32)
            dqt[j] += lax.dot_general(key, shifted, (((0,), (0,)), ((), ())), preferred_element_type=F32)
            return 0

        lax.fori_loop(begin, end, lag, 0)

    def arrived(j):
        await_bytes(lseb.at[j], r_l.at[j])
        await_bytes(dlb.at[j * 16 : (j + 1) * 16], r_d.at[j])
        await_bytes(qb.at[j * 128 : (j + 1) * 128], r_q.at[j])
        await_bytes(dob.at[j * 128 : (j + 1) * 128], r_do.at[j])

    def hand_back(j):
        for n in range(4):
            dqs[j * 128 : (j + 1) * 128, n * 128 : (n + 1) * 128] = dqt[j, :, n * 128 : (n + 1) * 128].T.astype(BF16)
        slot = 2 * g + core
        for e in (1, 0):
            src = dqs.at[pl.ds(pl.multiple_of(j * 128 + (zx(e) % 2) * 64, 64), 64)]
            dst = dqr.at[slot]
            if e or j:
                remote(src, dst, s_dq, r_dq, (zx(e), 4 * pair + block_of(j))).start()
            else:
                pltpu.make_async_copy(src, dst, r_dq).start()

    def to_partner(i):
        pxs[i] = acc[blk(2 * i + 1 - core)].astype(BF16)
        remote(pxs.at[i], pxr.at[i], s_px, r_px.at[i], partner).start()

    def from_partner(i):
        await_bytes(pxr.at[i], r_px.at[i])
        rts[i] = (acc[blk(2 * i + core)] + pxr[i].astype(F32)).astype(BF16)

    def send_back(off):
        for a in range(2):
            i = (2 * (1 - off)) + xx(a)
            for e in range(4):
                src = rts.at[i, pl.ds(pl.multiple_of(zx(e) * 64, 64), 64)]
                dst = ret.at[off * 8 + z * 2 + xq]
                if off == 0 and a == 0 and e == 0:
                    pltpu.make_async_copy(src, dst, r_rt).start()
                else:
                    remote(src, dst, s_rtp if off else s_rt, r_rtn if off else r_rt, (zx(e), at(-off, a, 0))).start()

    for j in range(2):
        arrived(j)
        work(j, block_of(j), block_of(j) + 5)
        hand_back(j)
    for j in range(2, 4):
        arrived(j)
        work(j, block_of(j), 4)
    for i in range(2):
        to_partner(i)
    work(2, 4, block_of(2) + 5)
    hand_back(2)
    for i in range(2):
        from_partner(i)

    @pl.when(jnp.logical_not(first))
    def _():
        send_back(1)

    work(3, 4, block_of(3) + 5)
    for i in range(2, 4):
        to_partner(i)
    hand_back(3)
    for i in range(2, 4):
        from_partner(i)
    send_back(0)

    await_bytes(ret.at[0:8], r_rt)

    @pl.when(last)
    def _():
        ret[8:16] = jnp.zeros((8, 64, 256), BF16)

    @pl.when(jnp.logical_not(last))
    def _():
        await_bytes(ret.at[8:16], r_rtn)

    for n in range(4):
        total = jnp.zeros((64, 256), F32)
        for off in range(2):
            for p in range(2):
                total = total + ret[off * 8 + (2 * p + n % 2) * 2 + n // 2].astype(F32)
        dk_ref[0, :, n * 128 : (n + 1) * 128] = total[:, 0:128].astype(BF16)
        dv_ref[0, :, n * 128 : (n + 1) * 128] = total[:, 128:256].astype(BF16)

    await_bytes(dqr, r_dq)
    for n in range(8):
        dq_ref[0, :, n * 512 : (n + 1) * 512] = dqr[n]

    await_bytes(kvb.at[0 : 7 * 64], s_kv)
    await_bytes(qb.at[0 : 7 * 64], s_q)
    await_bytes(dob.at[0 : 7 * 64], s_do)
    await_bytes(dqs.at[0 : 7 * 64], s_dq)
    await_bytes(pxs, s_px)
    await_bytes(ret.at[0:7], s_rt)
    await_bytes(dlb.at[0 : 7 * 8], s_d)
    for n in range(1, 4):
        await_bytes(lseb.at[0], s_l.at[n])

    @pl.when(to_x != xq)
    def _():
        await_bytes(lseb.at[0], s_l.at[0])

    @pl.when(jnp.logical_not(last))
    def _():
        await_bytes(kvb.at[0:512], s_kvn)

    @pl.when(first)
    def _():
        await_bytes(kvb.at[0:512], s_kvp)

    @pl.when(jnp.logical_not(first))
    def _():
        await_bytes(kvb.at[0:1024], s_kvp)
        await_bytes(ret.at[0:8], s_rtp)


def local(queries, keys, values, outputs, gradient, sums, lengths):
    vmem = pl.BlockSpec(memory_space=pltpu.VMEM)
    hbm = pl.BlockSpec(memory_space=pltpu.HBM)
    dma = pltpu.SemaphoreType.DMA
    return pl.pallas_call(
        kernel,
        out_shape=(
            jax.ShapeDtypeStruct((1, 64, 4096), BF16),
            jax.ShapeDtypeStruct((1, 64, 512), BF16),
            jax.ShapeDtypeStruct((1, 64, 512), BF16),
        ),
        in_specs=[hbm] * 6 + [pl.BlockSpec(memory_space=pltpu.SMEM)],
        out_specs=(vmem, vmem, vmem),
        scratch_shapes=[
            pltpu.VMEM((2, 64, 512), BF16),
            pltpu.VMEM((64, 4096), BF16),
            pltpu.VMEM((64, 4096), BF16),
            pltpu.VMEM((64, 1024), BF16),
            pltpu.VMEM((2048, 256), BF16),
            pltpu.VMEM((512, 512), BF16),
            pltpu.VMEM((512, 512), BF16),
            pltpu.VMEM((8, 256), F32),
            pltpu.VMEM((4, 8, 128), F32),
            pltpu.VMEM((4, 8, 128), F32),
            pltpu.VMEM((64, 128), F32),
            pltpu.VMEM((2048, 256), F32),
            pltpu.VMEM((4, 128, 512), F32),
            pltpu.VMEM((512, 512), BF16),
            pltpu.VMEM((8, 64, 512), BF16),
            pltpu.VMEM((4, 256, 256), BF16),
            pltpu.VMEM((4, 256, 256), BF16),
            pltpu.VMEM((4, 256, 256), BF16),
            pltpu.VMEM((16, 64, 256), BF16),
            dma((5,)), dma, dma, dma((8,)), dma, dma((8,)), dma, dma((4,)), dma, dma((4,)),
            dma((4,)), dma((4,)), dma, dma((4,)), dma, dma, dma, dma((4,)), dma, dma, dma, dma,
        ],
        compiler_params=pltpu.CompilerParams(
            collective_id=0, has_side_effects=True, vmem_limit_bytes=63 * 2**20
        ),
        name="attention_backward",
    )(queries, keys, values, outputs, gradient, jnp.transpose(sums, (0, 2, 1)), lengths)


def solution(mesh):
    in_specs = (
        P("ctx", "head", None),
        P("ctx", "head", None),
        P("ctx", "head", None),
        P("ctx", "head", None),
        P("ctx", "head", None),
        P("ctx", None, "head"),
        P(),
    )
    out_specs = (P("ctx", "head", None), P("ctx", "head", None), P("ctx", "head", None))
    return jax.shard_map(local, mesh=mesh, in_specs=in_specs, out_specs=out_specs, check_vma=False)
```

```python
import jax
import jax.numpy as jnp
from jax import lax
from jax.experimental import pallas as pl
from jax.experimental.pallas import tpu as pltpu
from jax.sharding import PartitionSpec as P

MESH = pl.DeviceIdType.MESH
F32 = jnp.float32
BF16 = jnp.bfloat16
SCALE = 128 ** (-0.5)
GROUPS = 16


def kernel(
    q_ref, k_ref, v_ref, o_ref, do_ref, lse_ref, len_ref,
    dq_ref, dk_ref, dv_ref,
    kin, ov, dov, kvs, kva, kvb, qb, dob, lset, lseb, dls, dlb, acc, dqt, dqs, dqr, pxs, pxr, rts, twin, via, ret,
    s_in, s_kv, s_kvn, r_kva, r_kvb, s_pa, r_pa, s_pb, r_pb, s_q, r_q, s_do, r_do,
    s_l, r_l, s_d, r_d, s_dq, r_dq, s_px, r_px, s_rt, s_rtp, r_rt, r_rtn, s_twin, r_twin, s_via, r_via,
):
    z = lax.axis_index("head")
    c = lax.axis_index("ctx")
    pair = c // 4
    own = c % 4
    xq = own // 2
    core = c % 2
    zb = z % 2
    zp = z // 2
    g = 2 * xq + zb
    first = pair == 0
    last = pair == GROUPS - 1
    before = pair == GROUPS // 2 - 1
    after = pair == GROUPS // 2
    bridge = before | after | first | last

    def zx(e):
        return (z, z + 1 - 2 * zb, (z + 2) % 4, 3 - z)[e]

    def xx(a):
        return xq if a == 0 else 1 - xq

    def kx(b):
        return core if b == 0 else 1 - core

    def at(off, a, b):
        return 4 * (pair + off) + 2 * xx(a) + kx(b)

    def remote(src, dst, ssem, rsem, dev):
        return pltpu.make_async_remote_copy(
            src_ref=src, dst_ref=dst, send_sem=ssem, recv_sem=rsem,
            device_id=dev, device_id_type=MESH,
        )

    def await_bytes(ref, sem):
        pltpu.make_async_copy(ref, ref, sem).wait()

    barrier = pltpu.get_barrier_semaphore()
    for a in range(2):
        for b in range(2):
            for e in range(4):
                if a or b or e:
                    pl.semaphore_signal(barrier, inc=1, device_id=(zx(e), at(0, a, b)), device_id_type=MESH)

    @pl.when(jnp.logical_not(first))
    def _():
        for a in range(2):
            for e in range(4):
                pl.semaphore_signal(barrier, inc=1, device_id=(zx(e), at(-1, a, 0)), device_id_type=MESH)

    @pl.when(jnp.logical_not(last))
    def _():
        for a in range(2):
            for e in range(4):
                pl.semaphore_signal(barrier, inc=1, device_id=(zx(e), at(1, a, 0)), device_id_type=MESH)

    def greet(e, to):
        pl.semaphore_signal(barrier, inc=1, device_id=(zx(e), to), device_id_type=MESH)

    across = own + 4 * jnp.where(before, GROUPS - 1, jnp.where(last, GROUPS // 2 - 1, jnp.where(after, 0, GROUPS // 2)))
    aside = 2 * (1 - xq) + core + 4 * jnp.where(before, 0, jnp.where(first, GROUPS // 2 - 1, jnp.where(after, GROUPS - 1, GROUPS // 2)))

    @pl.when(bridge)
    def _():
        for e in range(4):
            greet(e, across)
        greet(0, aside)

    loads = [
        pltpu.make_async_copy(src, dst, s_in.at[n])
        for n, (src, dst) in enumerate(
            ((k_ref.at[0], kin.at[0]), (v_ref.at[0], kin.at[1]), (lse_ref.at[0], lset), (do_ref.at[0], dov), (o_ref.at[0], ov))
        )
    ]
    for load in loads:
        load.start()
    acc[...] = jnp.zeros_like(acc)

    place = lax.broadcasted_iota(jnp.int32, (8, 128), 1) + (pair * 1024 + zp * 128)

    def block_of(j):
        return 2 * ((xq + j // 2) % 2) + (core + j % 2) % 2

    def seek(d, carry):
        begin, found = carry
        found = tuple(jnp.where(place + 256 * block_of(n) >= begin, begin, f) for n, f in enumerate(found))
        return begin + len_ref[d], found

    _, opens = lax.fori_loop(0, 64, seek, (jnp.int32(0), tuple(jnp.zeros((8, 128), jnp.int32) for _ in range(4))))

    for load in loads[:2]:
        load.wait()
    for n in range(4):
        kvs[:, n * 256 : n * 256 + 128] = kin[0, :, n * 128 : (n + 1) * 128]
        kvs[:, n * 256 + 128 : (n + 1) * 256] = kin[1, :, n * 128 : (n + 1) * 128]

    for load in loads[2:]:
        load.wait()
    lanes = lax.broadcasted_iota(jnp.int32, (64, 128), 1)
    delta = jnp.zeros((64, 128), F32)
    for n in range(32):
        part = dov[:, n * 128 : (n + 1) * 128].astype(F32) * ov[:, n * 128 : (n + 1) * 128].astype(F32)
        delta = jnp.where(lanes == n, jnp.sum(part, axis=1, keepdims=True), delta)
    both = jnp.concatenate([delta, delta], axis=0).T
    for n in range(4):
        dls[n] = both[n * 8 : (n + 1) * 8]

    pl.semaphore_wait(barrier, 15 + 8 * ((pair + GROUPS - 1) // GROUPS) + 8 * ((2 * GROUPS - 2 - pair) // GROUPS) + jnp.where(bridge, 5, 0))

    rows_own = pl.ds(pl.multiple_of(own * 256 + z * 64, 64), 64)

    def send_kv(off):
        for a in range(2):
            for e in range(4):
                there = 2 * xx(a) + zx(e) % 2
                src = kvs.at[:, pl.ds(pl.multiple_of(there * 256, 256), 256)]
                if off:
                    remote(src, kva.at[rows_own], s_kvn, r_kva.at[own], (zx(e), at(1, a, 0))).start()
                elif a or e:
                    remote(src, kvb.at[rows_own], s_kv, r_kvb.at[own], (zx(e), at(0, a, 0))).start()
                else:
                    pltpu.make_async_copy(src, kvb.at[rows_own], r_kvb.at[own]).start()

    @pl.when(before)
    def _():
        for e in range(4):
            src = kvs.at[:, pl.ds(pl.multiple_of((2 * xq + zx(e) % 2) * 256, 256), 256)]
            remote(src, kva.at[rows_own], s_kvn, r_kva.at[own], (zx(e), at(1, 0, 0))).start()
        src = kvs.at[:, pl.ds(pl.multiple_of((1 - xq) * 512, 512), 512)]
        remote(src, twin, s_twin, r_twin, (z, aside)).start()

    send_kv(0)

    @pl.when(jnp.logical_not(last | before))
    def _():
        send_kv(1)

    to_x = z // 2
    for e in (0, 2):
        half = zx(e) // 2
        for b in range(2):
            dev = (zx(e), 4 * pair + 2 * to_x + kx(b))
            slot = 2 * ((to_x + xq) % 2) + b
            src, dst = lset.at[:, pl.ds(pl.multiple_of(half * 128, 128), 128)], lseb.at[slot]
            if e == 0 and b == 0:
                @pl.when(to_x == xq)
                def _():
                    pltpu.make_async_copy(src, dst, r_l.at[slot]).start()

                @pl.when(to_x != xq)
                def _():
                    remote(src, dst, s_l.at[0], r_l.at[slot], dev).start()
            else:
                remote(src, dst, s_l.at[e + b], r_l.at[slot], dev).start()

    for a in range(2):
        for b in range(2):
            for e in range(2):
                src = dls.at[2 * xx(a) + zx(e) % 2]
                slot = 2 * a + b
                dst = dlb.at[pl.ds(pl.multiple_of(slot * 16 + zb * 8, 8), 8)]
                if a or b or e:
                    remote(src, dst, s_d, r_d.at[slot], (zx(e), at(0, a, b))).start()
                else:
                    pltpu.make_async_copy(src, dst, r_d.at[slot]).start()

    await_bytes(kvb.at[0 : 7 * 64], s_kv)
    for a in range(2):
        for b in range(2):
            for e in range(2):
                lane = (2 * xx(a) + zx(e) % 2) * 1024 + kx(b) * 512
                cols = pl.ds(pl.multiple_of(lane, 512), 512)
                for ref, buf, ss, rr in ((q_ref, qb, s_q, r_q), (do_ref, dob, s_do, r_do)):
                    src = ref.at[0, :, cols]
                    slot = 2 * a + b
                    dst = buf.at[pl.ds(pl.multiple_of(slot * 128 + zb * 64, 64), 64)]
                    if a or b or e:
                        remote(src, dst, ss, rr.at[slot], (zx(e), at(0, a, b))).start()
                    else:
                        pltpu.make_async_copy(src, dst, rr.at[slot]).start()

    for n in range(4):
        dqt[n] = jnp.zeros((128, 512), F32)
    def blk(b):
        return pl.ds(pl.multiple_of(b * 256, 256), 256)

    partner = (z, at(0, 0, 1))

    def hand_on(buf, sent, got, i):
        b = 2 * i + core
        remote(buf.at[blk(b)], buf.at[blk(b)], sent, got.at[b], partner).start()

    def own_blocks():
        for i in range(2):
            await_bytes(kvb.at[blk(2 * i + core)], r_kvb.at[2 * i + core])
            hand_on(kvb, s_pb, r_pb, i)
        for i in range(2):
            await_bytes(kvb.at[blk(2 * i + 1 - core)], r_pb.at[2 * i + 1 - core])

    def earlier_blocks():
        @pl.when(first)
        def _():
            kva[...] = jnp.zeros_like(kva)

        @pl.when(first)
        def _():
            await_bytes(twin, r_twin)
            theirs = 2 * (1 - xq) + core
            dst = kva.at[pl.ds(pl.multiple_of(theirs * 256 + z * 64, 64), 64)]
            for e in range(4):
                src = twin.at[:, pl.ds(pl.multiple_of(zx(e) % 2 * 256, 256), 256)]
                remote(src, dst, s_via, r_kva.at[theirs], (zx(e), across)).start()

        @pl.when(jnp.logical_not(first))
        def _():
            for i in range(2):
                await_bytes(kva.at[blk(2 * i + core)], r_kva.at[2 * i + core])
                hand_on(kva, s_pa, r_pa, i)
            for i in range(2):
                await_bytes(kva.at[blk(2 * i + 1 - core)], r_pa.at[2 * i + 1 - core])

    steps = lax.broadcasted_iota(jnp.int32, (256, 128), 0)
    low = lax.broadcasted_iota(jnp.int32, (8, 128), 1) < 64

    def work(j, buf):
        bi = block_of(j)
        ahead = 4 if buf is kvb else 0
        lse_all = lseb[j]
        delta_all = jnp.where(low, dlb[j * 16 : j * 16 + 8], dlb[j * 16 + 8 : j * 16 + 16])
        lse_mine = jnp.where(core == 0, lse_all[0:4], lse_all[4:8])
        delta_mine = jnp.where(core == 0, delta_all[0:4], delta_all[4:8])
        lse_row = jnp.concatenate([lse_mine[n : n + 1] for n in range(4)], axis=1)
        delta_row = jnp.concatenate([delta_mine[n : n + 1] for n in range(4)], axis=1)
        where_open = opens[j][0:1]
        where_here = (place + 256 * bi)[0:1]
        qp = qb[j * 128 : (j + 1) * 128]
        dop = dob[j * 128 : (j + 1) * 128]
        qm = jnp.concatenate([qp[:, n * 128 : (n + 1) * 128] for n in range(4)], axis=0)
        dom = jnp.concatenate([dop[:, n * 128 : (n + 1) * 128] for n in range(4)], axis=0)

        def lag(b, _):
            rows = blk(b + ahead)
            key = buf[blk(b), 0:128]
            value = buf[blk(b), 128:256]
            base = (4 * pair - 4 + ahead + b) * 256
            allowed = (steps >= where_open - base) & (steps <= where_here - base)
            allowed = jnp.concatenate([allowed] * 4, axis=1)
            scores = lax.dot_general(key, qm, (((1,), (1,)), ((), ())), preferred_element_type=F32)
            weights = jnp.where(allowed, jnp.exp(scores * SCALE - lse_row), 0.0)
            grads = lax.dot_general(value, dom, (((1,), (1,)), ((), ())), preferred_element_type=F32)
            shifted = (weights * (grads - delta_row) * SCALE).astype(BF16)
            acc[rows, 128:256] += jnp.dot(weights.astype(BF16), dom, preferred_element_type=F32)
            acc[rows, 0:128] += jnp.dot(shifted, qm, preferred_element_type=F32)
            dqt[j] += lax.dot_general(key, shifted, (((0,), (0,)), ((), ())), preferred_element_type=F32)
            return 0

        lax.fori_loop(0 if ahead else bi, bi + 1 if ahead else 4, lag, 0)

    def arrived(j):
        await_bytes(lseb.at[j], r_l.at[j])
        await_bytes(dlb.at[j * 16 : (j + 1) * 16], r_d.at[j])
        await_bytes(qb.at[j * 128 : (j + 1) * 128], r_q.at[j])
        await_bytes(dob.at[j * 128 : (j + 1) * 128], r_do.at[j])

    def hand_back(j):
        for n in range(4):
            dqs[j * 128 : (j + 1) * 128, n * 128 : (n + 1) * 128] = dqt[j, :, n * 128 : (n + 1) * 128].T.astype(BF16)
        slot = 2 * g + core
        for e in (1, 0):
            src = dqs.at[pl.ds(pl.multiple_of(j * 128 + (zx(e) % 2) * 64, 64), 64)]
            dst = dqr.at[slot]
            if e or j:
                remote(src, dst, s_dq, r_dq, (zx(e), 4 * pair + block_of(j))).start()
            else:
                pltpu.make_async_copy(src, dst, r_dq).start()

    def to_partner(i):
        pxs[i] = acc[blk(2 * i + 1 - core)].astype(BF16)
        remote(pxs.at[i], pxr.at[i], s_px, r_px.at[i], partner).start()

    def from_partner(i):
        await_bytes(pxr.at[i], r_px.at[i])
        rts[i] = (acc[blk(2 * i + core)] + pxr[i].astype(F32)).astype(BF16)

    def send_back(off):
        for a in range(2):
            i = (2 * (1 - off)) + xx(a)
            for e in range(4):
                src = rts.at[i, pl.ds(pl.multiple_of(zx(e) * 64, 64), 64)]
                dst = ret.at[off * 8 + xq * 4 + z]
                if off == 0 and a == 0 and e == 0:
                    pltpu.make_async_copy(src, dst, r_rt).start()
                else:
                    remote(src, dst, s_rtp if off else s_rt, r_rtn.at[xq] if off else r_rt, (zx(e), at(-off, a, 0))).start()

    own_blocks()
    for j in range(2):
        arrived(j)
        work(j, kvb)
    earlier_blocks()
    for j in range(2):
        work(j, kva)
        hand_back(j)
    for j in range(2, 4):
        arrived(j)
        work(j, kva)
    for i in range(2):
        to_partner(i)
    work(2, kvb)
    for i in range(2):
        from_partner(i)

    @pl.when(jnp.logical_not(first | after))
    def _():
        send_back(1)

    @pl.when(after)
    def _():
        for e in range(4):
            part = pl.ds(pl.multiple_of(zx(e) * 64, 64), 64)
            remote(rts.at[xq, part], ret.at[8 + xq * 4 + z], s_rtp, r_rtn.at[xq], (zx(e), at(-1, 0, 0))).start()
        remote(rts.at[1 - xq], via, s_twin, r_via, (z, aside)).start()

    hand_back(2)
    work(3, kvb)

    for i in range(2, 4):
        to_partner(i)
    hand_back(3)
    for i in range(2, 4):
        from_partner(i)
    send_back(0)

    @pl.when(last)
    def _():
        await_bytes(via, r_via)
        for e in range(4):
            src = via.at[pl.ds(pl.multiple_of(zx(e) * 64, 64), 64)]
            remote(src, ret.at[8 + (1 - xq) * 4 + z], s_via, r_rtn.at[1 - xq], (zx(e), across)).start()

    await_bytes(ret.at[0:8], r_rt)

    @pl.when(last)
    def _():
        ret[8:16] = jnp.zeros((8, 64, 256), BF16)

    @pl.when(jnp.logical_not(last))
    def _():
        await_bytes(ret.at[8:12], r_rtn.at[0])
        await_bytes(ret.at[12:16], r_rtn.at[1])

    for n in range(4):
        total = jnp.zeros((64, 256), F32)
        for off in range(2):
            for p in range(2):
                total = total + ret[off * 8 + (n // 2) * 4 + 2 * p + n % 2].astype(F32)
        dk_ref[0, :, n * 128 : (n + 1) * 128] = total[:, 0:128].astype(BF16)
        dv_ref[0, :, n * 128 : (n + 1) * 128] = total[:, 128:256].astype(BF16)

    await_bytes(dqr, r_dq)
    for n in range(8):
        dq_ref[0, :, n * 512 : (n + 1) * 512] = dqr[n]

    await_bytes(qb.at[0 : 7 * 64], s_q)
    await_bytes(dob.at[0 : 7 * 64], s_do)
    await_bytes(dqs.at[0 : 7 * 64], s_dq)
    await_bytes(pxs, s_px)
    await_bytes(ret.at[0:7], s_rt)
    await_bytes(dlb.at[0 : 7 * 8], s_d)
    for n in range(1, 4):
        await_bytes(lseb.at[0], s_l.at[n])

    @pl.when(to_x != xq)
    def _():
        await_bytes(lseb.at[0], s_l.at[0])

    @pl.when(before)
    def _():
        await_bytes(kvb.at[0:256], s_kvn)
        await_bytes(twin, s_twin)

    @pl.when(jnp.logical_not(last | before))
    def _():
        await_bytes(kvb.at[0:512], s_kvn)

    await_bytes(kvb.at[0:512], s_pb)

    @pl.when(jnp.logical_not(first))
    def _():
        await_bytes(kvb.at[0:512], s_pa)

    @pl.when(after)
    def _():
        await_bytes(ret.at[0:4], s_rtp)
        await_bytes(via, s_twin)

    @pl.when(jnp.logical_not(first | after))
    def _():
        await_bytes(ret.at[0:8], s_rtp)

    @pl.when(first | last)
    def _():
        await_bytes(via, s_via)


def local(queries, keys, values, outputs, gradient, sums, lengths):
    vmem = pl.BlockSpec(memory_space=pltpu.VMEM)
    hbm = pl.BlockSpec(memory_space=pltpu.HBM)
    dma = pltpu.SemaphoreType.DMA
    return pl.pallas_call(
        kernel,
        out_shape=(
            jax.ShapeDtypeStruct((1, 64, 4096), BF16),
            jax.ShapeDtypeStruct((1, 64, 512), BF16),
            jax.ShapeDtypeStruct((1, 64, 512), BF16),
        ),
        in_specs=[hbm] * 6 + [pl.BlockSpec(memory_space=pltpu.SMEM)],
        out_specs=(vmem, vmem, vmem),
        scratch_shapes=[
            pltpu.VMEM((2, 64, 512), BF16),
            pltpu.VMEM((64, 4096), BF16),
            pltpu.VMEM((64, 4096), BF16),
            pltpu.VMEM((64, 1024), BF16),
            pltpu.VMEM((1024, 256), BF16),
            pltpu.VMEM((1024, 256), BF16),
            pltpu.VMEM((512, 512), BF16),
            pltpu.VMEM((512, 512), BF16),
            pltpu.VMEM((8, 256), F32),
            pltpu.VMEM((4, 8, 128), F32),
            pltpu.VMEM((4, 8, 128), F32),
            pltpu.VMEM((64, 128), F32),
            pltpu.VMEM((2048, 256), F32),
            pltpu.VMEM((4, 128, 512), F32),
            pltpu.VMEM((512, 512), BF16),
            pltpu.VMEM((8, 64, 512), BF16),
            pltpu.VMEM((4, 256, 256), BF16),
            pltpu.VMEM((4, 256, 256), BF16),
            pltpu.VMEM((4, 256, 256), BF16),
            pltpu.VMEM((64, 512), BF16),
            pltpu.VMEM((256, 256), BF16),
            pltpu.VMEM((16, 64, 256), BF16),
            dma((5,)), dma, dma, dma((4,)), dma((4,)), dma, dma((4,)), dma, dma((4,)), dma, dma((4,)), dma, dma((4,)),
            dma((4,)), dma((4,)), dma, dma((4,)), dma, dma, dma, dma((4,)), dma, dma, dma, dma((2,)),
            dma, dma, dma, dma,
        ],
        compiler_params=pltpu.CompilerParams(
            collective_id=0, has_side_effects=True, vmem_limit_bytes=63 * 2**20
        ),
        name="attention_backward",
    )(queries, keys, values, outputs, gradient, jnp.transpose(sums, (0, 2, 1)), lengths)


def solution(mesh):
    in_specs = (
        P("ctx", "head", None),
        P("ctx", "head", None),
        P("ctx", "head", None),
        P("ctx", "head", None),
        P("ctx", "head", None),
        P("ctx", None, "head"),
        P(),
    )
    out_specs = (P("ctx", "head", None), P("ctx", "head", None), P("ctx", "head", None))
    return jax.shard_map(local, mesh=mesh, in_specs=in_specs, out_specs=out_specs, check_vma=False)
```

```python
import jax
import jax.numpy as jnp
from jax import lax
from jax.experimental import pallas as pl
from jax.experimental.pallas import tpu as pltpu
from jax.sharding import PartitionSpec as P

MESH = pl.DeviceIdType.MESH
F32 = jnp.float32
BF16 = jnp.bfloat16
SCALE = 128 ** (-0.5)
GROUPS = 16


def kernel(
    q_ref, k_ref, v_ref, o_ref, do_ref, lse_ref, len_ref,
    dq_ref, dk_ref, dv_ref,
    kin, ov, dov, kvs, kva, kvb, qb, dob, lset, lseb, dls, dlb, acc, dqt, dqs, dqr, pxs, pxr, rts, twin, via, ret,
    s_in, s_kv, s_kvn, r_kva, r_kvb, s_pa, r_pa, s_pb, r_pb, s_q, r_q, s_do, r_do,
    s_l, r_l, s_d, r_d, s_dq, r_dq, s_px, r_px, s_rt, s_rtp, r_rt, r_rtn, s_twin, r_twin, s_via, r_via,
):
    z = lax.axis_index("head")
    c = lax.axis_index("ctx")
    pair = c // 4
    own = c % 4
    xq = own // 2
    core = c % 2
    zb = z % 2
    zp = z // 2
    g = 2 * xq + zb
    first = pair == 0
    last = pair == GROUPS - 1
    before = pair == GROUPS // 2 - 1
    after = pair == GROUPS // 2
    bridge = before | after | first | last

    def zx(e):
        return (z, z + 1 - 2 * zb, (z + 2) % 4, 3 - z)[e]

    def xx(a):
        return xq if a == 0 else 1 - xq

    def kx(b):
        return core if b == 0 else 1 - core

    def at(off, a, b):
        return 4 * (pair + off) + 2 * xx(a) + kx(b)

    def remote(src, dst, ssem, rsem, dev):
        return pltpu.make_async_remote_copy(
            src_ref=src, dst_ref=dst, send_sem=ssem, recv_sem=rsem,
            device_id=dev, device_id_type=MESH,
        )

    def await_bytes(ref, sem):
        pltpu.make_async_copy(ref, ref, sem).wait()

    barrier = pltpu.get_barrier_semaphore()
    for a in range(2):
        for b in range(2):
            for e in range(4):
                if a or b or e:
                    pl.semaphore_signal(barrier, inc=1, device_id=(zx(e), at(0, a, b)), device_id_type=MESH)

    @pl.when(jnp.logical_not(first))
    def _():
        for a in range(2):
            for e in range(4):
                pl.semaphore_signal(barrier, inc=1, device_id=(zx(e), at(-1, a, 0)), device_id_type=MESH)

    @pl.when(jnp.logical_not(last))
    def _():
        for a in range(2):
            for e in range(4):
                pl.semaphore_signal(barrier, inc=1, device_id=(zx(e), at(1, a, 0)), device_id_type=MESH)

    def greet(e, to):
        pl.semaphore_signal(barrier, inc=1, device_id=(zx(e), to), device_id_type=MESH)

    across = own + 4 * jnp.where(before, GROUPS - 1, jnp.where(last, GROUPS // 2 - 1, jnp.where(after, 0, GROUPS // 2)))
    aside = 2 * (1 - xq) + core + 4 * jnp.where(before, 0, jnp.where(first, GROUPS // 2 - 1, jnp.where(after, GROUPS - 1, GROUPS // 2)))

    @pl.when(bridge)
    def _():
        for e in range(4):
            greet(e, across)
        greet(0, aside)

    loads = [
        pltpu.make_async_copy(src, dst, s_in.at[n])
        for n, (src, dst) in enumerate(
            ((k_ref.at[0], kin.at[0]), (v_ref.at[0], kin.at[1]), (lse_ref.at[0], lset), (do_ref.at[0], dov), (o_ref.at[0], ov))
        )
    ]
    for load in loads:
        load.start()
    acc[...] = jnp.zeros_like(acc)

    place = lax.broadcasted_iota(jnp.int32, (8, 128), 1) + (pair * 1024 + zp * 128)

    def block_of(j):
        return 2 * ((xq + j // 2) % 2) + (core + j % 2) % 2

    def seek(d, carry):
        begin, found = carry
        found = tuple(jnp.where(place + 256 * block_of(n) >= begin, begin, f) for n, f in enumerate(found))
        return begin + len_ref[d], found

    _, opens = lax.fori_loop(0, 64, seek, (jnp.int32(0), tuple(jnp.zeros((8, 128), jnp.int32) for _ in range(4))))

    for load in loads[:2]:
        load.wait()
    for n in range(4):
        kvs[:, n * 256 : n * 256 + 128] = kin[0, :, n * 128 : (n + 1) * 128]
        kvs[:, n * 256 + 128 : (n + 1) * 256] = kin[1, :, n * 128 : (n + 1) * 128]

    for load in loads[2:]:
        load.wait()
    lanes = lax.broadcasted_iota(jnp.int32, (64, 128), 1)
    delta = jnp.zeros((64, 128), F32)
    for n in range(32):
        part = dov[:, n * 128 : (n + 1) * 128].astype(F32) * ov[:, n * 128 : (n + 1) * 128].astype(F32)
        delta = jnp.where(lanes == n, jnp.sum(part, axis=1, keepdims=True), delta)
    both = jnp.concatenate([delta, delta], axis=0).T
    for n in range(4):
        dls[n] = both[n * 8 : (n + 1) * 8]

    pl.semaphore_wait(barrier, 15 + 8 * ((pair + GROUPS - 1) // GROUPS) + 8 * ((2 * GROUPS - 2 - pair) // GROUPS) + jnp.where(bridge, 5, 0))

    rows_own = pl.ds(pl.multiple_of(own * 256 + z * 64, 64), 64)

    def send_kv(off, a, e):
        there = 2 * xx(a) + zx(e) % 2
        src = kvs.at[:, pl.ds(pl.multiple_of(there * 256, 256), 256)]
        if off:
            remote(src, kva.at[rows_own], s_kvn, r_kva.at[own], (zx(e), at(1, a, 0))).start()
        elif a or e:
            remote(src, kvb.at[rows_own], s_kv, r_kvb.at[own], (zx(e), at(0, a, 0))).start()
        else:
            pltpu.make_async_copy(src, kvb.at[rows_own], r_kvb.at[own]).start()

    @pl.when(before)
    def _():
        for e in range(4):
            src = kvs.at[:, pl.ds(pl.multiple_of((2 * xq + zx(e) % 2) * 256, 256), 256)]
            remote(src, kva.at[rows_own], s_kvn, r_kva.at[own], (zx(e), at(1, 0, 0))).start()
        src = kvs.at[:, pl.ds(pl.multiple_of((1 - xq) * 512, 512), 512)]
        remote(src, twin, s_twin, r_twin, (z, aside)).start()

    for a, e in ((0, 0), (0, 2), (1, 0), (0, 3), (1, 2), (0, 1), (1, 3), (1, 1)):
        send_kv(0, a, e)

    @pl.when(jnp.logical_not(last | before))
    def _():
        for a, e in ((0, 2), (1, 2), (0, 3), (1, 3), (0, 0), (0, 1), (1, 0), (1, 1)):
            send_kv(1, a, e)

    to_x = z // 2
    for e in (0, 2):
        half = zx(e) // 2
        for b in range(2):
            dev = (zx(e), 4 * pair + 2 * to_x + kx(b))
            slot = 2 * ((to_x + xq) % 2) + b
            src, dst = lset.at[:, pl.ds(pl.multiple_of(half * 128, 128), 128)], lseb.at[slot]
            if e == 0 and b == 0:
                @pl.when(to_x == xq)
                def _():
                    pltpu.make_async_copy(src, dst, r_l.at[slot]).start()

                @pl.when(to_x != xq)
                def _():
                    remote(src, dst, s_l.at[0], r_l.at[slot], dev).start()
            else:
                remote(src, dst, s_l.at[e + b], r_l.at[slot], dev).start()

    for a in range(2):
        for b in range(2):
            for e in range(2):
                src = dls.at[2 * xx(a) + zx(e) % 2]
                slot = 2 * a + b
                dst = dlb.at[pl.ds(pl.multiple_of(slot * 16 + zb * 8, 8), 8)]
                if a or b or e:
                    remote(src, dst, s_d, r_d.at[slot], (zx(e), at(0, a, b))).start()
                else:
                    pltpu.make_async_copy(src, dst, r_d.at[slot]).start()

    def send_queries(*which):
        for a, b, e in which:
            lane = (2 * xx(a) + zx(e) % 2) * 1024 + kx(b) * 512
            cols = pl.ds(pl.multiple_of(lane, 512), 512)
            for ref, buf, ss, rr in ((q_ref, qb, s_q, r_q), (do_ref, dob, s_do, r_do)):
                src = ref.at[0, :, cols]
                slot = 2 * a + b
                dst = buf.at[pl.ds(pl.multiple_of(slot * 128 + zb * 64, 64), 64)]
                if a or b or e:
                    remote(src, dst, ss, rr.at[slot], (zx(e), at(0, a, b))).start()
                else:
                    pltpu.make_async_copy(src, dst, rr.at[slot]).start()

    send_queries((0, 0, 0), (0, 1, 0))

    @pl.when(first)
    def _():
        await_bytes(twin, r_twin)
        theirs = 2 * (1 - xq) + core
        dst = kva.at[pl.ds(pl.multiple_of(theirs * 256 + z * 64, 64), 64)]
        for e in range(4):
            src = twin.at[:, pl.ds(pl.multiple_of(zx(e) % 2 * 256, 256), 256)]
            remote(src, dst, s_via, r_kva.at[theirs], (zx(e), across)).start()

    send_queries((0, 0, 1), (1, 0, 0), (0, 1, 1), (1, 1, 0), (1, 0, 1), (1, 1, 1))
    await_bytes(kvb.at[0 : 7 * 64], s_kv)

    for n in range(4):
        dqt[n] = jnp.zeros((128, 512), F32)
    def blk(b):
        return pl.ds(pl.multiple_of(b * 256, 256), 256)

    partner = (z, at(0, 0, 1))

    def hand_on(buf, sent, got, i):
        b = 2 * i + core
        remote(buf.at[blk(b)], buf.at[blk(b)], sent, got.at[b], partner).start()

    def own_blocks():
        for i in range(2):
            await_bytes(kvb.at[blk(2 * i + core)], r_kvb.at[2 * i + core])
            hand_on(kvb, s_pb, r_pb, i)
        for i in range(2):
            await_bytes(kvb.at[blk(2 * i + 1 - core)], r_pb.at[2 * i + 1 - core])

    def earlier_blocks():
        @pl.when(first)
        def _():
            kva[...] = jnp.zeros_like(kva)

        @pl.when(jnp.logical_not(first))
        def _():
            for i in range(2):
                await_bytes(kva.at[blk(2 * i + core)], r_kva.at[2 * i + core])
                hand_on(kva, s_pa, r_pa, i)
            for i in range(2):
                await_bytes(kva.at[blk(2 * i + 1 - core)], r_pa.at[2 * i + 1 - core])

    steps = lax.broadcasted_iota(jnp.int32, (256, 128), 0)
    low = lax.broadcasted_iota(jnp.int32, (8, 128), 1) < 64

    def work(j, buf, count=None):
        bi = block_of(j)
        ahead = 4 if buf is kvb else 0
        lse_all = lseb[j]
        delta_all = jnp.where(low, dlb[j * 16 : j * 16 + 8], dlb[j * 16 + 8 : j * 16 + 16])
        lse_mine = jnp.where(core == 0, lse_all[0:4], lse_all[4:8])
        delta_mine = jnp.where(core == 0, delta_all[0:4], delta_all[4:8])
        lse_row = jnp.concatenate([lse_mine[n : n + 1] for n in range(4)], axis=1)
        delta_row = jnp.concatenate([delta_mine[n : n + 1] for n in range(4)], axis=1)
        where_open = opens[j][0:1]
        where_here = (place + 256 * bi)[0:1]
        qp = qb[j * 128 : (j + 1) * 128]
        dop = dob[j * 128 : (j + 1) * 128]
        qm = jnp.concatenate([qp[:, n * 128 : (n + 1) * 128] for n in range(4)], axis=0)
        dom = jnp.concatenate([dop[:, n * 128 : (n + 1) * 128] for n in range(4)], axis=0)

        def lag(b, _):
            rows = blk(b + ahead)
            key = buf[blk(b), 0:128]
            value = buf[blk(b), 128:256]
            base = (4 * pair - 4 + ahead + b) * 256
            allowed = (steps >= where_open - base) & (steps <= where_here - base)
            allowed = jnp.concatenate([allowed] * 4, axis=1)
            scores = lax.dot_general(key, qm, (((1,), (1,)), ((), ())), preferred_element_type=F32)
            weights = jnp.where(allowed, jnp.exp(scores * SCALE - lse_row), 0.0)
            grads = lax.dot_general(value, dom, (((1,), (1,)), ((), ())), preferred_element_type=F32)
            shifted = (weights * (grads - delta_row) * SCALE).astype(BF16)
            acc[rows, 128:256] += jnp.dot(weights.astype(BF16), dom, preferred_element_type=F32)
            acc[rows, 0:128] += jnp.dot(shifted, qm, preferred_element_type=F32)
            dqt[j] += lax.dot_general(key, shifted, (((0,), (0,)), ((), ())), preferred_element_type=F32)
            return 0

        lax.fori_loop(0 if ahead else bi, (bi + 1 if count is None else count) if ahead else 4, lag, 0)

    def arrived(j):
        await_bytes(lseb.at[j], r_l.at[j])
        await_bytes(dlb.at[j * 16 : (j + 1) * 16], r_d.at[j])
        await_bytes(qb.at[j * 128 : (j + 1) * 128], r_q.at[j])
        await_bytes(dob.at[j * 128 : (j + 1) * 128], r_do.at[j])

    def hand_back(j):
        for n in range(4):
            dqs[j * 128 : (j + 1) * 128, n * 128 : (n + 1) * 128] = dqt[j, :, n * 128 : (n + 1) * 128].T.astype(BF16)
        slot = 2 * g + core
        for e in (1, 0):
            src = dqs.at[pl.ds(pl.multiple_of(j * 128 + (zx(e) % 2) * 64, 64), 64)]
            dst = dqr.at[slot]
            if e or j:
                remote(src, dst, s_dq, r_dq, (zx(e), 4 * pair + block_of(j))).start()
            else:
                pltpu.make_async_copy(src, dst, r_dq).start()

    def to_partner(i):
        pxs[i] = acc[blk(2 * i + 1 - core)].astype(BF16)
        remote(pxs.at[i], pxr.at[i], s_px, r_px.at[i], partner).start()

    def from_partner(i):
        await_bytes(pxr.at[i], r_px.at[i])
        rts[i] = (acc[blk(2 * i + core)] + pxr[i].astype(F32)).astype(BF16)

    def send_back(off):
        for a in range(2):
            i = (2 * (1 - off)) + xx(a)
            for e in range(4):
                src = rts.at[i, pl.ds(pl.multiple_of(zx(e) * 64, 64), 64)]
                dst = ret.at[off * 8 + xq * 4 + z]
                if off == 0 and a == 0 and e == 0:
                    pltpu.make_async_copy(src, dst, r_rt).start()
                else:
                    remote(src, dst, s_rtp if off else s_rt, r_rtn.at[xq] if off else r_rt, (zx(e), at(-off, a, 0))).start()

    own_blocks()
    for j in range(2):
        arrived(j)
        work(j, kvb)
    earlier_blocks()
    for j in range(2):
        work(j, kva)
        hand_back(j)
    for j in range(2, 4):
        arrived(j)
        work(j, kva)
    for i in range(2):
        to_partner(i)
    pieces_left = block_of(2) + 1
    work(2, kvb, jnp.where(after, 0, pieces_left))
    for i in range(2):
        from_partner(i)

    @pl.when(jnp.logical_not(first | after))
    def _():
        send_back(1)

    @pl.when(after)
    def _():
        for e in range(4):
            part = pl.ds(pl.multiple_of(zx(e) * 64, 64), 64)
            remote(rts.at[xq, part], ret.at[8 + xq * 4 + z], s_rtp, r_rtn.at[xq], (zx(e), at(-1, 0, 0))).start()
        remote(rts.at[1 - xq], via, s_twin, r_via, (z, aside)).start()

    @pl.when(after)
    def _():
        work(2, kvb)

    hand_back(2)
    work(3, kvb)

    for i in range(2, 4):
        to_partner(i)
    hand_back(3)
    for i in range(2, 4):
        from_partner(i)
    send_back(0)

    @pl.when(last)
    def _():
        await_bytes(via, r_via)
        for e in range(4):
            src = via.at[pl.ds(pl.multiple_of(zx(e) * 64, 64), 64)]
            remote(src, ret.at[8 + (1 - xq) * 4 + z], s_via, r_rtn.at[1 - xq], (zx(e), across)).start()

    await_bytes(dqr, r_dq)
    for n in range(8):
        dq_ref[0, :, n * 512 : (n + 1) * 512] = dqr[n]
    await_bytes(ret.at[0:8], r_rt)

    @pl.when(last)
    def _():
        ret[8:16] = jnp.zeros((8, 64, 256), BF16)

    @pl.when(jnp.logical_not(last))
    def _():
        await_bytes(ret.at[8:12], r_rtn.at[0])
        await_bytes(ret.at[12:16], r_rtn.at[1])

    for n in range(4):
        total = jnp.zeros((64, 256), F32)
        for off in range(2):
            for p in range(2):
                total = total + ret[off * 8 + (n // 2) * 4 + 2 * p + n % 2].astype(F32)
        dk_ref[0, :, n * 128 : (n + 1) * 128] = total[:, 0:128].astype(BF16)
        dv_ref[0, :, n * 128 : (n + 1) * 128] = total[:, 128:256].astype(BF16)


    await_bytes(qb.at[0 : 7 * 64], s_q)
    await_bytes(dob.at[0 : 7 * 64], s_do)
    await_bytes(dqs.at[0 : 7 * 64], s_dq)
    await_bytes(pxs, s_px)
    await_bytes(ret.at[0:7], s_rt)
    await_bytes(dlb.at[0 : 7 * 8], s_d)
    for n in range(1, 4):
        await_bytes(lseb.at[0], s_l.at[n])

    @pl.when(to_x != xq)
    def _():
        await_bytes(lseb.at[0], s_l.at[0])

    @pl.when(before)
    def _():
        await_bytes(kvb.at[0:256], s_kvn)
        await_bytes(twin, s_twin)

    @pl.when(jnp.logical_not(last | before))
    def _():
        await_bytes(kvb.at[0:512], s_kvn)

    await_bytes(kvb.at[0:512], s_pb)

    @pl.when(jnp.logical_not(first))
    def _():
        await_bytes(kvb.at[0:512], s_pa)

    @pl.when(after)
    def _():
        await_bytes(ret.at[0:4], s_rtp)
        await_bytes(via, s_twin)

    @pl.when(jnp.logical_not(first | after))
    def _():
        await_bytes(ret.at[0:8], s_rtp)

    @pl.when(first | last)
    def _():
        await_bytes(via, s_via)


def local(queries, keys, values, outputs, gradient, sums, lengths):
    vmem = pl.BlockSpec(memory_space=pltpu.VMEM)
    hbm = pl.BlockSpec(memory_space=pltpu.HBM)
    dma = pltpu.SemaphoreType.DMA
    return pl.pallas_call(
        kernel,
        out_shape=(
            jax.ShapeDtypeStruct((1, 64, 4096), BF16),
            jax.ShapeDtypeStruct((1, 64, 512), BF16),
            jax.ShapeDtypeStruct((1, 64, 512), BF16),
        ),
        in_specs=[hbm] * 6 + [pl.BlockSpec(memory_space=pltpu.SMEM)],
        out_specs=(vmem, vmem, vmem),
        scratch_shapes=[
            pltpu.VMEM((2, 64, 512), BF16),
            pltpu.VMEM((64, 4096), BF16),
            pltpu.VMEM((64, 4096), BF16),
            pltpu.VMEM((64, 1024), BF16),
            pltpu.VMEM((1024, 256), BF16),
            pltpu.VMEM((1024, 256), BF16),
            pltpu.VMEM((512, 512), BF16),
            pltpu.VMEM((512, 512), BF16),
            pltpu.VMEM((8, 256), F32),
            pltpu.VMEM((4, 8, 128), F32),
            pltpu.VMEM((4, 8, 128), F32),
            pltpu.VMEM((64, 128), F32),
            pltpu.VMEM((2048, 256), F32),
            pltpu.VMEM((4, 128, 512), F32),
            pltpu.VMEM((512, 512), BF16),
            pltpu.VMEM((8, 64, 512), BF16),
            pltpu.VMEM((4, 256, 256), BF16),
            pltpu.VMEM((4, 256, 256), BF16),
            pltpu.VMEM((4, 256, 256), BF16),
            pltpu.VMEM((64, 512), BF16),
            pltpu.VMEM((256, 256), BF16),
            pltpu.VMEM((16, 64, 256), BF16),
            dma((5,)), dma, dma, dma((4,)), dma((4,)), dma, dma((4,)), dma, dma((4,)), dma, dma((4,)), dma, dma((4,)),
            dma((4,)), dma((4,)), dma, dma((4,)), dma, dma, dma, dma((4,)), dma, dma, dma, dma((2,)),
            dma, dma, dma, dma,
        ],
        compiler_params=pltpu.CompilerParams(
            collective_id=0, has_side_effects=True, vmem_limit_bytes=63 * 2**20
        ),
        name="attention_backward",
    )(queries, keys, values, outputs, gradient, jnp.transpose(sums, (0, 2, 1)), lengths)


def solution(mesh):
    in_specs = (
        P("ctx", "head", None),
        P("ctx", "head", None),
        P("ctx", "head", None),
        P("ctx", "head", None),
        P("ctx", "head", None),
        P("ctx", None, "head"),
        P(),
    )
    out_specs = (P("ctx", "head", None), P("ctx", "head", None), P("ctx", "head", None))
    return jax.shard_map(local, mesh=mesh, in_specs=in_specs, out_specs=out_specs, check_vma=False)
```

```python
import jax
import jax.numpy as jnp
from jax import lax
from jax.experimental import pallas as pl
from jax.experimental.pallas import tpu as pltpu
from jax.sharding import PartitionSpec as P

MESH = pl.DeviceIdType.MESH
F32 = jnp.float32
BF16 = jnp.bfloat16
SCALE = 128 ** (-0.5)
GROUPS = 16


def kernel(
    q_ref, k_ref, v_ref, o_ref, do_ref, lse_ref, len_ref,
    dq_ref, dk_ref, dv_ref,
    kin, ov, dov, kvs, kva, kvb, qb, dob, lset, lseb, dls, dlb, acc, dqt, dqs, dqr, pxs, pxr, rts, twin, via, ret,
    s_in, s_kv, s_kvn, r_kva, r_kvb, s_pa, r_pa, s_pb, r_pb, s_q, r_q, s_do, r_do,
    s_l, r_l, s_d, r_d, s_dq, r_dq, s_px, r_px, s_rt, s_rtp, r_rt, r_rtn, s_twin, r_twin, s_via, r_via,
):
    z = lax.axis_index("head")
    c = lax.axis_index("ctx")
    pair = c // 4
    own = c % 4
    xq = own // 2
    core = c % 2
    zb = z % 2
    zp = z // 2
    g = 2 * xq + zb
    first = pair == 0
    last = pair == GROUPS - 1
    before = pair == GROUPS // 2 - 1
    after = pair == GROUPS // 2
    bridge = before | after | first | last

    def zx(e):
        return (z, z + 1 - 2 * zb, (z + 2) % 4, 3 - z)[e]

    def xx(a):
        return xq if a == 0 else 1 - xq

    def kx(b):
        return core if b == 0 else 1 - core

    def at(off, a, b):
        return 4 * (pair + off) + 2 * xx(a) + kx(b)

    def remote(src, dst, ssem, rsem, dev):
        return pltpu.make_async_remote_copy(
            src_ref=src, dst_ref=dst, send_sem=ssem, recv_sem=rsem,
            device_id=dev, device_id_type=MESH,
        )

    def await_bytes(ref, sem):
        pltpu.make_async_copy(ref, ref, sem).wait()

    barrier = pltpu.get_barrier_semaphore()
    for a in range(2):
        for b in range(2):
            for e in range(4):
                if a or b or e:
                    pl.semaphore_signal(barrier, inc=1, device_id=(zx(e), at(0, a, b)), device_id_type=MESH)

    @pl.when(jnp.logical_not(first))
    def _():
        for a in range(2):
            for e in range(4):
                pl.semaphore_signal(barrier, inc=1, device_id=(zx(e), at(-1, a, 0)), device_id_type=MESH)

    @pl.when(jnp.logical_not(last))
    def _():
        for a in range(2):
            for e in range(4):
                pl.semaphore_signal(barrier, inc=1, device_id=(zx(e), at(1, a, 0)), device_id_type=MESH)

    def greet(e, to):
        pl.semaphore_signal(barrier, inc=1, device_id=(zx(e), to), device_id_type=MESH)

    across = own + 4 * jnp.where(before, GROUPS - 1, jnp.where(last, GROUPS // 2 - 1, jnp.where(after, 0, GROUPS // 2)))
    aside = 2 * (1 - xq) + core + 4 * jnp.where(before, 0, jnp.where(first, GROUPS // 2 - 1, jnp.where(after, GROUPS - 1, GROUPS // 2)))

    @pl.when(bridge)
    def _():
        for e in range(4):
            greet(e, across)
        greet(0, aside)

    loads = [
        pltpu.make_async_copy(src, dst, s_in.at[n])
        for n, (src, dst) in enumerate(
            ((k_ref.at[0], kin.at[0]), (v_ref.at[0], kin.at[1]), (lse_ref.at[0], lset), (do_ref.at[0], dov), (o_ref.at[0], ov))
        )
    ]
    for load in loads:
        load.start()
    acc[...] = jnp.zeros_like(acc)

    place = lax.broadcasted_iota(jnp.int32, (8, 128), 1) + (pair * 1024 + zp * 128)

    def block_of(j):
        return 2 * ((xq + j // 2) % 2) + (core + j % 2) % 2

    def seek(d, carry):
        begin, found = carry
        found = tuple(jnp.where(place + 256 * block_of(n) >= begin, begin, f) for n, f in enumerate(found))
        return begin + len_ref[d], found

    _, opens = lax.fori_loop(0, 64, seek, (jnp.int32(0), tuple(jnp.zeros((8, 128), jnp.int32) for _ in range(4))))

    for load in loads[:2]:
        load.wait()
    for n in range(4):
        kvs[:, n * 256 : n * 256 + 128] = kin[0, :, n * 128 : (n + 1) * 128]
        kvs[:, n * 256 + 128 : (n + 1) * 256] = kin[1, :, n * 128 : (n + 1) * 128]

    for load in loads[2:]:
        load.wait()
    lanes = lax.broadcasted_iota(jnp.int32, (64, 128), 1)
    delta = jnp.zeros((64, 128), F32)
    for n in range(32):
        part = dov[:, n * 128 : (n + 1) * 128].astype(F32) * ov[:, n * 128 : (n + 1) * 128].astype(F32)
        delta = jnp.where(lanes == n, jnp.sum(part, axis=1, keepdims=True), delta)
    both = jnp.concatenate([delta, delta], axis=0).T
    for n in range(4):
        dls[n] = both[n * 8 : (n + 1) * 8]

    pl.semaphore_wait(barrier, 15 + 8 * ((pair + GROUPS - 1) // GROUPS) + 8 * ((2 * GROUPS - 2 - pair) // GROUPS) + jnp.where(bridge, 5, 0))

    rows_own = pl.ds(pl.multiple_of(own * 256 + z * 64, 64), 64)

    def send_kv(off, a, e):
        there = 2 * xx(a) + zx(e) % 2
        src = kvs.at[:, pl.ds(pl.multiple_of(there * 256, 256), 256)]
        if off:
            remote(src, kva.at[rows_own], s_kvn, r_kva.at[own], (zx(e), at(1, a, 0))).start()
        elif a or e:
            remote(src, kvb.at[rows_own], s_kv, r_kvb.at[own], (zx(e), at(0, a, 0))).start()
        else:
            pltpu.make_async_copy(src, kvb.at[rows_own], r_kvb.at[own]).start()

    @pl.when(before)
    def _():
        for e in range(4):
            src = kvs.at[:, pl.ds(pl.multiple_of((2 * xq + zx(e) % 2) * 256, 256), 256)]
            remote(src, kva.at[rows_own], s_kvn, r_kva.at[own], (zx(e), at(1, 0, 0))).start()
        src = kvs.at[:, pl.ds(pl.multiple_of((1 - xq) * 512, 512), 512)]
        remote(src, twin, s_twin, r_twin, (z, aside)).start()

    for a, e in ((0, 0), (0, 2), (1, 0), (0, 3), (1, 2), (0, 1), (1, 3), (1, 1)):
        send_kv(0, a, e)

    @pl.when(jnp.logical_not(last | before))
    def _():
        for a, e in ((0, 2), (1, 2), (0, 3), (1, 3), (0, 0), (0, 1), (1, 0), (1, 1)):
            send_kv(1, a, e)

    to_x = z // 2
    for e in (0, 2):
        half = zx(e) // 2
        for b in range(2):
            dev = (zx(e), 4 * pair + 2 * to_x + kx(b))
            slot = 2 * ((to_x + xq) % 2) + b
            src, dst = lset.at[:, pl.ds(pl.multiple_of(half * 128, 128), 128)], lseb.at[slot]
            if e == 0 and b == 0:
                @pl.when(to_x == xq)
                def _():
                    pltpu.make_async_copy(src, dst, r_l.at[slot]).start()

                @pl.when(to_x != xq)
                def _():
                    remote(src, dst, s_l.at[0], r_l.at[slot], dev).start()
            else:
                remote(src, dst, s_l.at[e + b], r_l.at[slot], dev).start()

    for a in range(2):
        for b in range(2):
            for e in range(2):
                src = dls.at[2 * xx(a) + zx(e) % 2]
                slot = 2 * a + b
                dst = dlb.at[pl.ds(pl.multiple_of(slot * 16 + zb * 8, 8), 8)]
                if a or b or e:
                    remote(src, dst, s_d, r_d.at[slot], (zx(e), at(0, a, b))).start()
                else:
                    pltpu.make_async_copy(src, dst, r_d.at[slot]).start()

    def send_queries(*which):
        for a, b, e in which:
            lane = (2 * xx(a) + zx(e) % 2) * 1024 + kx(b) * 512
            cols = pl.ds(pl.multiple_of(lane, 512), 512)
            for ref, buf, ss, rr in ((q_ref, qb, s_q, r_q), (do_ref, dob, s_do, r_do)):
                src = ref.at[0, :, cols]
                slot = 2 * a + b
                dst = buf.at[pl.ds(pl.multiple_of(slot * 128 + zb * 64, 64), 64)]
                if a or b or e:
                    remote(src, dst, ss, rr.at[slot], (zx(e), at(0, a, b))).start()
                else:
                    pltpu.make_async_copy(src, dst, rr.at[slot]).start()

    send_queries((0, 0, 0), (0, 1, 0), (1, 0, 0), (1, 1, 0), (0, 0, 1), (0, 1, 1))

    @pl.when(first)
    def _():
        await_bytes(twin, r_twin)
        theirs = 2 * (1 - xq) + core
        dst = kva.at[pl.ds(pl.multiple_of(theirs * 256 + z * 64, 64), 64)]
        for e in range(4):
            src = twin.at[:, pl.ds(pl.multiple_of(zx(e) % 2 * 256, 256), 256)]
            remote(src, dst, s_via, r_kva.at[theirs], (zx(e), across)).start()

    send_queries((1, 0, 1), (1, 1, 1))
    await_bytes(kvb.at[0 : 7 * 64], s_kv)

    for n in range(4):
        dqt[n] = jnp.zeros((128, 512), F32)
    def blk(b):
        return pl.ds(pl.multiple_of(b * 256, 256), 256)

    partner = (z, at(0, 0, 1))

    def hand_on(buf, sent, got, i):
        b = 2 * i + core
        remote(buf.at[blk(b)], buf.at[blk(b)], sent, got.at[b], partner).start()

    def own_blocks():
        for i in range(2):
            await_bytes(kvb.at[blk(2 * i + core)], r_kvb.at[2 * i + core])
            hand_on(kvb, s_pb, r_pb, i)
        for i in range(2):
            await_bytes(kvb.at[blk(2 * i + 1 - core)], r_pb.at[2 * i + 1 - core])

    def earlier_blocks():
        @pl.when(first)
        def _():
            kva[...] = jnp.zeros_like(kva)

        @pl.when(jnp.logical_not(first))
        def _():
            for i in range(2):
                await_bytes(kva.at[blk(2 * i + core)], r_kva.at[2 * i + core])
                hand_on(kva, s_pa, r_pa, i)
            for i in range(2):
                await_bytes(kva.at[blk(2 * i + 1 - core)], r_pa.at[2 * i + 1 - core])

    steps = lax.broadcasted_iota(jnp.int32, (256, 128), 0)
    low = lax.broadcasted_iota(jnp.int32, (8, 128), 1) < 64

    def work(j, buf, count=None):
        bi = block_of(j)
        ahead = 4 if buf is kvb else 0
        lse_all = lseb[j]
        delta_all = jnp.where(low, dlb[j * 16 : j * 16 + 8], dlb[j * 16 + 8 : j * 16 + 16])
        lse_mine = jnp.where(core == 0, lse_all[0:4], lse_all[4:8])
        delta_mine = jnp.where(core == 0, delta_all[0:4], delta_all[4:8])
        lse_row = jnp.concatenate([lse_mine[n : n + 1] for n in range(4)], axis=1)
        delta_row = jnp.concatenate([delta_mine[n : n + 1] for n in range(4)], axis=1)
        where_open = opens[j][0:1]
        where_here = (place + 256 * bi)[0:1]
        qp = qb[j * 128 : (j + 1) * 128]
        dop = dob[j * 128 : (j + 1) * 128]
        qm = jnp.concatenate([qp[:, n * 128 : (n + 1) * 128] for n in range(4)], axis=0)
        dom = jnp.concatenate([dop[:, n * 128 : (n + 1) * 128] for n in range(4)], axis=0)

        def lag(b, _):
            rows = blk(b + ahead)
            key = buf[blk(b), 0:128]
            value = buf[blk(b), 128:256]
            base = (4 * pair - 4 + ahead + b) * 256
            allowed = (steps >= where_open - base) & (steps <= where_here - base)
            allowed = jnp.concatenate([allowed] * 4, axis=1)
            scores = lax.dot_general(key, qm, (((1,), (1,)), ((), ())), preferred_element_type=F32)
            weights = jnp.where(allowed, jnp.exp(scores * SCALE - lse_row), 0.0)
            grads = lax.dot_general(value, dom, (((1,), (1,)), ((), ())), preferred_element_type=F32)
            shifted = (weights * (grads - delta_row) * SCALE).astype(BF16)
            acc[rows, 128:256] += jnp.dot(weights.astype(BF16), dom, preferred_element_type=F32)
            acc[rows, 0:128] += jnp.dot(shifted, qm, preferred_element_type=F32)
            dqt[j] += lax.dot_general(key, shifted, (((0,), (0,)), ((), ())), preferred_element_type=F32)
            return 0

        lax.fori_loop(0 if ahead else bi, (bi + 1 if count is None else count) if ahead else 4, lag, 0)

    def arrived(j):
        await_bytes(lseb.at[j], r_l.at[j])
        await_bytes(dlb.at[j * 16 : (j + 1) * 16], r_d.at[j])
        await_bytes(qb.at[j * 128 : (j + 1) * 128], r_q.at[j])
        await_bytes(dob.at[j * 128 : (j + 1) * 128], r_do.at[j])

    def hand_back(j):
        for n in range(4):
            dqs[j * 128 : (j + 1) * 128, n * 128 : (n + 1) * 128] = dqt[j, :, n * 128 : (n + 1) * 128].T.astype(BF16)
        slot = 2 * g + core
        for e in (1, 0):
            src = dqs.at[pl.ds(pl.multiple_of(j * 128 + (zx(e) % 2) * 64, 64), 64)]
            dst = dqr.at[slot]
            if e or j:
                remote(src, dst, s_dq, r_dq, (zx(e), 4 * pair + block_of(j))).start()
            else:
                pltpu.make_async_copy(src, dst, r_dq).start()

    def to_partner(i):
        pxs[i] = acc[blk(2 * i + 1 - core)].astype(BF16)
        remote(pxs.at[i], pxr.at[i], s_px, r_px.at[i], partner).start()

    def from_partner(i):
        await_bytes(pxr.at[i], r_px.at[i])
        rts[i] = (acc[blk(2 * i + core)] + pxr[i].astype(F32)).astype(BF16)

    def send_back(off):
        for a in range(2):
            i = (2 * (1 - off)) + xx(a)
            for e in range(4):
                src = rts.at[i, pl.ds(pl.multiple_of(zx(e) * 64, 64), 64)]
                dst = ret.at[off * 8 + xq * 4 + z]
                if off == 0 and a == 0 and e == 0:
                    pltpu.make_async_copy(src, dst, r_rt).start()
                else:
                    remote(src, dst, s_rtp if off else s_rt, r_rtn.at[xq] if off else r_rt, (zx(e), at(-off, a, 0))).start()

    own_blocks()
    for j in range(2):
        arrived(j)
        work(j, kvb)
    earlier_blocks()
    for j in range(2):
        work(j, kva)
        hand_back(j)
    for j in range(2, 4):
        arrived(j)
        work(j, kva)
    for i in range(2):
        to_partner(i)
    pieces_left = block_of(2) + 1
    work(2, kvb, jnp.where(after, 0, pieces_left))
    for i in range(2):
        from_partner(i)

    @pl.when(jnp.logical_not(first | after))
    def _():
        send_back(1)

    @pl.when(after)
    def _():
        for e in range(4):
            part = pl.ds(pl.multiple_of(zx(e) * 64, 64), 64)
            remote(rts.at[xq, part], ret.at[8 + xq * 4 + z], s_rtp, r_rtn.at[xq], (zx(e), at(-1, 0, 0))).start()
        remote(rts.at[1 - xq], via, s_twin, r_via, (z, aside)).start()

    @pl.when(after)
    def _():
        work(2, kvb)

    hand_back(2)
    work(3, kvb)

    for i in range(2, 4):
        to_partner(i)
    hand_back(3)
    for i in range(2, 4):
        from_partner(i)
    send_back(0)

    @pl.when(last)
    def _():
        await_bytes(via, r_via)
        for e in range(4):
            src = via.at[pl.ds(pl.multiple_of(zx(e) * 64, 64), 64)]
            remote(src, ret.at[8 + (1 - xq) * 4 + z], s_via, r_rtn.at[1 - xq], (zx(e), across)).start()

    await_bytes(dqr, r_dq)
    for n in range(8):
        dq_ref[0, :, n * 512 : (n + 1) * 512] = dqr[n]
    await_bytes(ret.at[0:8], r_rt)

    @pl.when(last)
    def _():
        ret[8:16] = jnp.zeros((8, 64, 256), BF16)

    @pl.when(jnp.logical_not(last))
    def _():
        await_bytes(ret.at[8:12], r_rtn.at[0])
        await_bytes(ret.at[12:16], r_rtn.at[1])

    for n in range(4):
        total = jnp.zeros((64, 256), F32)
        for off in range(2):
            for p in range(2):
                total = total + ret[off * 8 + (n // 2) * 4 + 2 * p + n % 2].astype(F32)
        dk_ref[0, :, n * 128 : (n + 1) * 128] = total[:, 0:128].astype(BF16)
        dv_ref[0, :, n * 128 : (n + 1) * 128] = total[:, 128:256].astype(BF16)


    await_bytes(qb.at[0 : 7 * 64], s_q)
    await_bytes(dob.at[0 : 7 * 64], s_do)
    await_bytes(dqs.at[0 : 7 * 64], s_dq)
    await_bytes(pxs, s_px)
    await_bytes(ret.at[0:7], s_rt)
    await_bytes(dlb.at[0 : 7 * 8], s_d)
    for n in range(1, 4):
        await_bytes(lseb.at[0], s_l.at[n])

    @pl.when(to_x != xq)
    def _():
        await_bytes(lseb.at[0], s_l.at[0])

    @pl.when(before)
    def _():
        await_bytes(kvb.at[0:256], s_kvn)
        await_bytes(twin, s_twin)

    @pl.when(jnp.logical_not(last | before))
    def _():
        await_bytes(kvb.at[0:512], s_kvn)

    await_bytes(kvb.at[0:512], s_pb)

    @pl.when(jnp.logical_not(first))
    def _():
        await_bytes(kvb.at[0:512], s_pa)

    @pl.when(after)
    def _():
        await_bytes(ret.at[0:4], s_rtp)
        await_bytes(via, s_twin)

    @pl.when(jnp.logical_not(first | after))
    def _():
        await_bytes(ret.at[0:8], s_rtp)

    @pl.when(first | last)
    def _():
        await_bytes(via, s_via)


def settle(dq_in, dk_in, dv_in, dq_ref, dk_ref, dv_ref, dq_held, dk_held, dv_held, s_in, s_out):
    moves = [(dk_in, dk_held, dk_ref), (dv_in, dv_held, dv_ref)]
    for n in range(4):
        rows = slice(n * 16, (n + 1) * 16)
        moves.append((dq_in.at[:, rows], dq_held.at[:, rows], dq_ref.at[:, rows]))
    came = [pltpu.make_async_copy(src, held, s_in.at[n]) for n, (src, held, _) in enumerate(moves)]
    goes = [pltpu.make_async_copy(held, dst, s_out.at[n]) for n, (_, held, dst) in enumerate(moves)]
    for copy in came:
        copy.start()
    for one, other in zip(came, goes):
        one.wait()
        other.start()
    for copy in goes:
        copy.wait()


def local(queries, keys, values, outputs, gradient, sums, lengths):
    vmem = pl.BlockSpec(memory_space=pltpu.VMEM)
    hbm = pl.BlockSpec(memory_space=pltpu.HBM)
    dma = pltpu.SemaphoreType.DMA
    made = pl.pallas_call(
        kernel,
        out_shape=(
            jax.ShapeDtypeStruct((1, 64, 4096), BF16),
            jax.ShapeDtypeStruct((1, 64, 512), BF16),
            jax.ShapeDtypeStruct((1, 64, 512), BF16),
        ),
        in_specs=[hbm] * 6 + [pl.BlockSpec(memory_space=pltpu.SMEM)],
        out_specs=(vmem, vmem, vmem),
        scratch_shapes=[
            pltpu.VMEM((2, 64, 512), BF16),
            pltpu.VMEM((64, 4096), BF16),
            pltpu.VMEM((64, 4096), BF16),
            pltpu.VMEM((64, 1024), BF16),
            pltpu.VMEM((1024, 256), BF16),
            pltpu.VMEM((1024, 256), BF16),
            pltpu.VMEM((512, 512), BF16),
            pltpu.VMEM((512, 512), BF16),
            pltpu.VMEM((8, 256), F32),
            pltpu.VMEM((4, 8, 128), F32),
            pltpu.VMEM((4, 8, 128), F32),
            pltpu.VMEM((64, 128), F32),
            pltpu.VMEM((2048, 256), F32),
            pltpu.VMEM((4, 128, 512), F32),
            pltpu.VMEM((512, 512), BF16),
            pltpu.VMEM((8, 64, 512), BF16),
            pltpu.VMEM((4, 256, 256), BF16),
            pltpu.VMEM((4, 256, 256), BF16),
            pltpu.VMEM((4, 256, 256), BF16),
            pltpu.VMEM((64, 512), BF16),
            pltpu.VMEM((256, 256), BF16),
            pltpu.VMEM((16, 64, 256), BF16),
            dma((5,)), dma, dma, dma((4,)), dma((4,)), dma, dma((4,)), dma, dma((4,)), dma, dma((4,)), dma, dma((4,)),
            dma((4,)), dma((4,)), dma, dma((4,)), dma, dma, dma, dma((4,)), dma, dma, dma, dma((2,)),
            dma, dma, dma, dma,
        ],
        compiler_params=pltpu.CompilerParams(
            collective_id=0, has_side_effects=True, vmem_limit_bytes=63 * 2**20
        ),
        name="attention_backward",
    )(queries, keys, values, outputs, gradient, jnp.transpose(sums, (0, 2, 1)), lengths)
    return pl.pallas_call(
        settle,
        out_shape=tuple(jax.ShapeDtypeStruct(m.shape, m.dtype) for m in made),
        in_specs=[hbm] * 3,
        out_specs=(hbm,) * 3,
        scratch_shapes=[pltpu.VMEM(m.shape, m.dtype) for m in made] + [dma((6,)), dma((6,))],
        compiler_params=pltpu.CompilerParams(vmem_limit_bytes=63 * 2**20),
        name="settle",
    )(*made)


def solution(mesh):
    in_specs = (
        P("ctx", "head", None),
        P("ctx", "head", None),
        P("ctx", "head", None),
        P("ctx", "head", None),
        P("ctx", "head", None),
        P("ctx", None, "head"),
        P(),
    )
    out_specs = (P("ctx", "head", None), P("ctx", "head", None), P("ctx", "head", None))
    return jax.shard_map(local, mesh=mesh, in_specs=in_specs, out_specs=out_specs, check_vma=False)
```

```python
import jax
import jax.numpy as jnp
from jax import lax
from jax.experimental import pallas as pl
from jax.experimental.pallas import tpu as pltpu
from jax.sharding import PartitionSpec as P

MESH = pl.DeviceIdType.MESH
F32 = jnp.float32
BF16 = jnp.bfloat16
SCALE = 128 ** (-0.5)
LOG2E = 1.4426950408889634
GROUPS = 16


def kernel(
    q_ref, k_ref, v_ref, o_ref, do_ref, lse_ref, len_ref,
    dq_ref, dk_ref, dv_ref,
    kin, ov, dov, kvs, kva, kvb, qb, dob, lset, lseb, dls, dlb, acc, dqt, dqs, dqr, pxs, pxr, rts, twin, via, ret,
    s_in, s_kv, s_kvn, r_kva, r_kvb, s_pa, r_pa, s_pb, r_pb, s_q, r_q, s_do, r_do,
    s_l, r_l, s_d, r_d, s_dq, r_dq, s_px, r_px, s_rt, s_rtp, r_rt, r_rtn, s_twin, r_twin, s_via, r_via,
):
    z = lax.axis_index("head")
    c = lax.axis_index("ctx")
    pair = c // 4
    own = c % 4
    xq = own // 2
    core = c % 2
    zb = z % 2
    zp = z // 2
    g = 2 * xq + zb
    first = pair == 0
    last = pair == GROUPS - 1
    before = pair == GROUPS // 2 - 1
    after = pair == GROUPS // 2
    bridge = before | after | first | last

    def zx(e):
        return (z, z + 1 - 2 * zb, (z + 2) % 4, 3 - z)[e]

    def xx(a):
        return xq if a == 0 else 1 - xq

    def kx(b):
        return core if b == 0 else 1 - core

    def at(off, a, b):
        return 4 * (pair + off) + 2 * xx(a) + kx(b)

    def remote(src, dst, ssem, rsem, dev):
        return pltpu.make_async_remote_copy(
            src_ref=src, dst_ref=dst, send_sem=ssem, recv_sem=rsem,
            device_id=dev, device_id_type=MESH,
        )

    def await_bytes(ref, sem):
        pltpu.make_async_copy(ref, ref, sem).wait()

    barrier = pltpu.get_barrier_semaphore()
    for a in range(2):
        for b in range(2):
            for e in range(4):
                if a or b or e:
                    pl.semaphore_signal(barrier, inc=1, device_id=(zx(e), at(0, a, b)), device_id_type=MESH)

    @pl.when(jnp.logical_not(first))
    def _():
        for a in range(2):
            for e in range(4):
                pl.semaphore_signal(barrier, inc=1, device_id=(zx(e), at(-1, a, 0)), device_id_type=MESH)

    @pl.when(jnp.logical_not(last))
    def _():
        for a in range(2):
            for e in range(4):
                pl.semaphore_signal(barrier, inc=1, device_id=(zx(e), at(1, a, 0)), device_id_type=MESH)

    def greet(e, to):
        pl.semaphore_signal(barrier, inc=1, device_id=(zx(e), to), device_id_type=MESH)

    across = own + 4 * jnp.where(before, GROUPS - 1, jnp.where(last, GROUPS // 2 - 1, jnp.where(after, 0, GROUPS // 2)))
    aside = 2 * (1 - xq) + core + 4 * jnp.where(before, 0, jnp.where(first, GROUPS // 2 - 1, jnp.where(after, GROUPS - 1, GROUPS // 2)))

    @pl.when(bridge)
    def _():
        for e in range(4):
            greet(e, across)
        greet(0, aside)

    loads = [
        pltpu.make_async_copy(src, dst, s_in.at[n])
        for n, (src, dst) in enumerate(
            ((k_ref.at[0], kin.at[0]), (v_ref.at[0], kin.at[1]), (lse_ref.at[0], lset), (do_ref.at[0], dov), (o_ref.at[0], ov))
        )
    ]
    for load in loads:
        load.start()
    acc[...] = jnp.zeros_like(acc)

    place = lax.broadcasted_iota(jnp.int32, (8, 128), 1) + (pair * 1024 + zp * 128)

    def block_of(j):
        return 2 * ((xq + j // 2) % 2) + (core + j % 2) % 2

    def seek(d, carry):
        begin, found = carry
        found = tuple(jnp.where(place + 256 * block_of(n) >= begin, begin, f) for n, f in enumerate(found))
        return begin + len_ref[d], found

    _, opens = lax.fori_loop(0, 64, seek, (jnp.int32(0), tuple(jnp.zeros((8, 128), jnp.int32) for _ in range(4))))

    for load in loads[:2]:
        load.wait()
    for n in range(4):
        kvs[:, n * 256 : n * 256 + 128] = kin[0, :, n * 128 : (n + 1) * 128]
        kvs[:, n * 256 + 128 : (n + 1) * 256] = kin[1, :, n * 128 : (n + 1) * 128]

    for load in loads[2:]:
        load.wait()
    lanes = lax.broadcasted_iota(jnp.int32, (64, 128), 1)
    delta = jnp.zeros((64, 128), F32)
    for n in range(32):
        part = dov[:, n * 128 : (n + 1) * 128].astype(F32) * ov[:, n * 128 : (n + 1) * 128].astype(F32)
        delta = jnp.where(lanes == n, jnp.sum(part, axis=1, keepdims=True), delta)
    both = jnp.concatenate([delta, delta], axis=0).T
    for n in range(4):
        dls[n] = both[n * 8 : (n + 1) * 8]

    pl.semaphore_wait(barrier, 15 + 8 * ((pair + GROUPS - 1) // GROUPS) + 8 * ((2 * GROUPS - 2 - pair) // GROUPS) + jnp.where(bridge, 5, 0))

    rows_own = pl.ds(pl.multiple_of(own * 256 + z * 64, 64), 64)

    def send_kv(off, a, e):
        there = 2 * xx(a) + zx(e) % 2
        src = kvs.at[:, pl.ds(pl.multiple_of(there * 256, 256), 256)]
        if off:
            remote(src, kva.at[rows_own], s_kvn, r_kva.at[own], (zx(e), at(1, a, 0))).start()
        elif a or e:
            remote(src, kvb.at[rows_own], s_kv, r_kvb.at[own], (zx(e), at(0, a, 0))).start()
        else:
            pltpu.make_async_copy(src, kvb.at[rows_own], r_kvb.at[own]).start()

    @pl.when(before)
    def _():
        for e in range(4):
            src = kvs.at[:, pl.ds(pl.multiple_of((2 * xq + zx(e) % 2) * 256, 256), 256)]
            remote(src, kva.at[rows_own], s_kvn, r_kva.at[own], (zx(e), at(1, 0, 0))).start()
        src = kvs.at[:, pl.ds(pl.multiple_of((1 - xq) * 512, 512), 512)]
        remote(src, twin, s_twin, r_twin, (z, aside)).start()

    for a, e in ((0, 0), (0, 2), (1, 0), (0, 3), (1, 2), (0, 1), (1, 3), (1, 1)):
        send_kv(0, a, e)

    @pl.when(jnp.logical_not(last | before))
    def _():
        for a, e in ((0, 2), (1, 2), (0, 3), (1, 3), (0, 0), (0, 1), (1, 0), (1, 1)):
            send_kv(1, a, e)

    to_x = z // 2
    for e in (0, 2):
        half = zx(e) // 2
        for b in range(2):
            dev = (zx(e), 4 * pair + 2 * to_x + kx(b))
            slot = 2 * ((to_x + xq) % 2) + b
            src, dst = lset.at[:, pl.ds(pl.multiple_of(half * 128, 128), 128)], lseb.at[slot]
            if e == 0 and b == 0:
                @pl.when(to_x == xq)
                def _():
                    pltpu.make_async_copy(src, dst, r_l.at[slot]).start()

                @pl.when(to_x != xq)
                def _():
                    remote(src, dst, s_l.at[0], r_l.at[slot], dev).start()
            else:
                remote(src, dst, s_l.at[e + b], r_l.at[slot], dev).start()

    for a in range(2):
        for b in range(2):
            for e in range(2):
                src = dls.at[2 * xx(a) + zx(e) % 2]
                slot = 2 * a + b
                dst = dlb.at[pl.ds(pl.multiple_of(slot * 16 + zb * 8, 8), 8)]
                if a or b or e:
                    remote(src, dst, s_d, r_d.at[slot], (zx(e), at(0, a, b))).start()
                else:
                    pltpu.make_async_copy(src, dst, r_d.at[slot]).start()

    def send_queries(*which):
        for a, b, e in which:
            lane = (2 * xx(a) + zx(e) % 2) * 1024 + kx(b) * 512
            cols = pl.ds(pl.multiple_of(lane, 512), 512)
            for ref, buf, ss, rr in ((q_ref, qb, s_q, r_q), (do_ref, dob, s_do, r_do)):
                src = ref.at[0, :, cols]
                slot = 2 * a + b
                dst = buf.at[pl.ds(pl.multiple_of(slot * 128 + zb * 64, 64), 64)]
                if a or b or e:
                    remote(src, dst, ss, rr.at[slot], (zx(e), at(0, a, b))).start()
                else:
                    pltpu.make_async_copy(src, dst, rr.at[slot]).start()

    send_queries((0, 0, 0), (0, 1, 0), (1, 0, 0), (1, 1, 0), (0, 0, 1), (0, 1, 1))

    @pl.when(first)
    def _():
        await_bytes(twin, r_twin)
        theirs = 2 * (1 - xq) + core
        dst = kva.at[pl.ds(pl.multiple_of(theirs * 256 + z * 64, 64), 64)]
        for e in range(4):
            src = twin.at[:, pl.ds(pl.multiple_of(zx(e) % 2 * 256, 256), 256)]
            remote(src, dst, s_via, r_kva.at[theirs], (zx(e), across)).start()

    send_queries((1, 0, 1), (1, 1, 1))
    await_bytes(kvb.at[0 : 7 * 64], s_kv)

    for n in range(4):
        dqt[n] = jnp.zeros((128, 512), F32)
    def blk(b):
        return pl.ds(pl.multiple_of(b * 256, 256), 256)

    partner = (z, at(0, 0, 1))

    def hand_on(buf, sent, got, i):
        b = 2 * i + core
        remote(buf.at[blk(b)], buf.at[blk(b)], sent, got.at[b], partner).start()

    def own_blocks():
        for i in range(2):
            await_bytes(kvb.at[blk(2 * i + core)], r_kvb.at[2 * i + core])
            hand_on(kvb, s_pb, r_pb, i)
        for i in range(2):
            await_bytes(kvb.at[blk(2 * i + 1 - core)], r_pb.at[2 * i + 1 - core])

    def earlier_blocks():
        @pl.when(first)
        def _():
            kva[...] = jnp.zeros_like(kva)

        @pl.when(jnp.logical_not(first))
        def _():
            for i in range(2):
                await_bytes(kva.at[blk(2 * i + core)], r_kva.at[2 * i + core])
                hand_on(kva, s_pa, r_pa, i)
            for i in range(2):
                await_bytes(kva.at[blk(2 * i + 1 - core)], r_pa.at[2 * i + 1 - core])

    steps = lax.broadcasted_iota(jnp.int32, (256, 128), 0)
    low = lax.broadcasted_iota(jnp.int32, (8, 128), 1) < 64

    def work(j, buf, begin, end):
        bi = block_of(j)
        ahead = 4 if buf is kvb else 0
        lse_all = lseb[j]
        delta_all = jnp.where(low, dlb[j * 16 : j * 16 + 8], dlb[j * 16 + 8 : j * 16 + 16])
        lse_mine = jnp.where(core == 0, lse_all[0:4], lse_all[4:8])
        delta_mine = jnp.where(core == 0, delta_all[0:4], delta_all[4:8])
        lse_row = jnp.concatenate([lse_mine[n : n + 1] for n in range(4)], axis=1) * LOG2E
        delta_row = jnp.concatenate([delta_mine[n : n + 1] for n in range(4)], axis=1)
        where_open = opens[j][0:1]
        where_here = (place + 256 * bi)[0:1]
        qp = qb[j * 128 : (j + 1) * 128]
        dop = dob[j * 128 : (j + 1) * 128]
        qm = jnp.concatenate([qp[:, n * 128 : (n + 1) * 128] for n in range(4)], axis=0)
        dom = jnp.concatenate([dop[:, n * 128 : (n + 1) * 128] for n in range(4)], axis=0)

        def lag(b, _):
            rows = blk(b + ahead)
            key = buf[blk(b), 0:128]
            value = buf[blk(b), 128:256]
            base = (4 * pair - 4 + ahead + b) * 256
            allowed = (steps >= where_open - base) & (steps <= where_here - base)
            allowed = jnp.concatenate([allowed] * 4, axis=1)
            scores = lax.dot_general(key, qm, (((1,), (1,)), ((), ())), preferred_element_type=F32)
            weights = jnp.where(allowed, jnp.exp2(scores * (SCALE * LOG2E) - lse_row), 0.0)
            grads = lax.dot_general(value, dom, (((1,), (1,)), ((), ())), preferred_element_type=F32)
            shifted = (weights * (grads - delta_row) * SCALE).astype(BF16)
            acc[rows, 128:256] += jnp.dot(weights.astype(BF16), dom, preferred_element_type=F32)
            acc[rows, 0:128] += jnp.dot(shifted, qm, preferred_element_type=F32)
            dqt[j] += lax.dot_general(key, shifted, (((0,), (0,)), ((), ())), preferred_element_type=F32)
            return 0

        lax.fori_loop(begin, end, lag, 0)

    def arrived(j):
        await_bytes(lseb.at[j], r_l.at[j])
        await_bytes(dlb.at[j * 16 : (j + 1) * 16], r_d.at[j])
        await_bytes(qb.at[j * 128 : (j + 1) * 128], r_q.at[j])
        await_bytes(dob.at[j * 128 : (j + 1) * 128], r_do.at[j])

    def hand_back(j):
        for n in range(4):
            dqs[j * 128 : (j + 1) * 128, n * 128 : (n + 1) * 128] = dqt[j, :, n * 128 : (n + 1) * 128].T.astype(BF16)
        slot = 2 * g + core
        for e in (1, 0):
            src = dqs.at[pl.ds(pl.multiple_of(j * 128 + (zx(e) % 2) * 64, 64), 64)]
            dst = dqr.at[slot]
            if e or j:
                remote(src, dst, s_dq, r_dq, (zx(e), 4 * pair + block_of(j))).start()
            else:
                pltpu.make_async_copy(src, dst, r_dq).start()

    def to_partner(i):
        pxs[i] = acc[blk(2 * i + 1 - core)].astype(BF16)
        remote(pxs.at[i], pxr.at[i], s_px, r_px.at[i], partner).start()

    def from_partner(i):
        await_bytes(pxr.at[i], r_px.at[i])
        rts[i] = (acc[blk(2 * i + core)] + pxr[i].astype(F32)).astype(BF16)

    def send_back():
        for a in range(2):
            for e in range(4):
                src = rts.at[xx(a), pl.ds(pl.multiple_of(zx(e) * 64, 64), 64)]
                remote(src, ret.at[8 + xq * 4 + z], s_rtp, r_rtn.at[xq], (zx(e), at(-1, a, 0))).start()

    def send_own(i):
        for e in (2, 3, 1, 0):
            src = rts.at[i, pl.ds(pl.multiple_of(zx(e) * 64, 64), 64)]
            dst = ret.at[xq * 4 + z]
            far = remote(src, dst, s_rt, r_rt, (zx(e), 4 * pair + 2 * (i - 2) + core))
            if e:
                far.start()
            else:
                pl.when(xq != i - 2)(far.start)
                pl.when(xq == i - 2)(pltpu.make_async_copy(src, dst, r_rt).start)

    own_blocks()
    for j in range(2):
        arrived(j)
        work(j, kvb, 0, block_of(j) + 1)
    earlier_blocks()
    for j in range(2):
        work(j, kva, block_of(j), 4)
        hand_back(j)
    for j in range(2, 4):
        arrived(j)
        work(j, kva, block_of(j), 4)
    for i in range(2):
        to_partner(i)
    reach = tuple(jnp.minimum(block_of(j) + 1, 2) for j in (2, 3))
    work(2, kvb, 0, jnp.where(after, 0, reach[0]))
    for i in range(2):
        from_partner(i)

    @pl.when(jnp.logical_not(first | after))
    def _():
        send_back()

    @pl.when(after)
    def _():
        for e in range(4):
            part = pl.ds(pl.multiple_of(zx(e) * 64, 64), 64)
            remote(rts.at[xq, part], ret.at[8 + xq * 4 + z], s_rtp, r_rtn.at[xq], (zx(e), at(-1, 0, 0))).start()
        remote(rts.at[1 - xq], via, s_twin, r_via, (z, aside)).start()

    @pl.when(after)
    def _():
        work(2, kvb, 0, reach[0])

    work(3, kvb, 0, reach[1])
    to_partner(2)
    work(2, kvb, 2, block_of(2) + 1)
    hand_back(2)
    from_partner(2)
    send_own(2)
    work(3, kvb, 2, block_of(3) + 1)
    to_partner(3)
    hand_back(3)
    from_partner(3)
    send_own(3)

    @pl.when(last)
    def _():
        await_bytes(via, r_via)
        for e in range(4):
            src = via.at[pl.ds(pl.multiple_of(zx(e) * 64, 64), 64)]
            remote(src, ret.at[8 + (1 - xq) * 4 + z], s_via, r_rtn.at[1 - xq], (zx(e), across)).start()

    await_bytes(dqr, r_dq)
    for n in range(8):
        dq_ref[0, :, n * 512 : (n + 1) * 512] = dqr[n]
    await_bytes(ret.at[0:8], r_rt)

    @pl.when(last)
    def _():
        ret[8:16] = jnp.zeros((8, 64, 256), BF16)

    @pl.when(jnp.logical_not(last))
    def _():
        await_bytes(ret.at[8:12], r_rtn.at[0])
        await_bytes(ret.at[12:16], r_rtn.at[1])

    for n in range(4):
        total = jnp.zeros((64, 256), F32)
        for off in range(2):
            for p in range(2):
                total = total + ret[off * 8 + (n // 2) * 4 + 2 * p + n % 2].astype(F32)
        dk_ref[0, :, n * 128 : (n + 1) * 128] = total[:, 0:128].astype(BF16)
        dv_ref[0, :, n * 128 : (n + 1) * 128] = total[:, 128:256].astype(BF16)


    await_bytes(qb.at[0 : 7 * 64], s_q)
    await_bytes(dob.at[0 : 7 * 64], s_do)
    await_bytes(dqs.at[0 : 7 * 64], s_dq)
    await_bytes(pxs, s_px)
    await_bytes(ret.at[0:7], s_rt)
    await_bytes(dlb.at[0 : 7 * 8], s_d)
    for n in range(1, 4):
        await_bytes(lseb.at[0], s_l.at[n])

    @pl.when(to_x != xq)
    def _():
        await_bytes(lseb.at[0], s_l.at[0])

    @pl.when(before)
    def _():
        await_bytes(kvb.at[0:256], s_kvn)
        await_bytes(twin, s_twin)

    @pl.when(jnp.logical_not(last | before))
    def _():
        await_bytes(kvb.at[0:512], s_kvn)

    await_bytes(kvb.at[0:512], s_pb)

    @pl.when(jnp.logical_not(first))
    def _():
        await_bytes(kvb.at[0:512], s_pa)

    @pl.when(after)
    def _():
        await_bytes(ret.at[0:4], s_rtp)
        await_bytes(via, s_twin)

    @pl.when(jnp.logical_not(first | after))
    def _():
        await_bytes(ret.at[0:8], s_rtp)

    @pl.when(first | last)
    def _():
        await_bytes(via, s_via)


def settle(dq_in, dk_in, dv_in, dq_ref, dk_ref, dv_ref, dq_held, dk_held, dv_held, s_in, s_out):
    moves = [(dk_in, dk_held, dk_ref), (dv_in, dv_held, dv_ref)]
    for n in range(4):
        rows = slice(n * 16, (n + 1) * 16)
        moves.append((dq_in.at[:, rows], dq_held.at[:, rows], dq_ref.at[:, rows]))
    came = [pltpu.make_async_copy(src, held, s_in.at[n]) for n, (src, held, _) in enumerate(moves)]
    goes = [pltpu.make_async_copy(held, dst, s_out.at[n]) for n, (_, held, dst) in enumerate(moves)]
    for copy in came:
        copy.start()
    for one, other in zip(came, goes):
        one.wait()
        other.start()
    for copy in goes:
        copy.wait()


def local(queries, keys, values, outputs, gradient, sums, lengths):
    vmem = pl.BlockSpec(memory_space=pltpu.VMEM)
    hbm = pl.BlockSpec(memory_space=pltpu.HBM)
    dma = pltpu.SemaphoreType.DMA
    made = pl.pallas_call(
        kernel,
        out_shape=(
            jax.ShapeDtypeStruct((1, 64, 4096), BF16),
            jax.ShapeDtypeStruct((1, 64, 512), BF16),
            jax.ShapeDtypeStruct((1, 64, 512), BF16),
        ),
        in_specs=[hbm] * 6 + [pl.BlockSpec(memory_space=pltpu.SMEM)],
        out_specs=(vmem, vmem, vmem),
        scratch_shapes=[
            pltpu.VMEM((2, 64, 512), BF16),
            pltpu.VMEM((64, 4096), BF16),
            pltpu.VMEM((64, 4096), BF16),
            pltpu.VMEM((64, 1024), BF16),
            pltpu.VMEM((1024, 256), BF16),
            pltpu.VMEM((1024, 256), BF16),
            pltpu.VMEM((512, 512), BF16),
            pltpu.VMEM((512, 512), BF16),
            pltpu.VMEM((8, 256), F32),
            pltpu.VMEM((4, 8, 128), F32),
            pltpu.VMEM((4, 8, 128), F32),
            pltpu.VMEM((64, 128), F32),
            pltpu.VMEM((2048, 256), F32),
            pltpu.VMEM((4, 128, 512), F32),
            pltpu.VMEM((512, 512), BF16),
            pltpu.VMEM((8, 64, 512), BF16),
            pltpu.VMEM((4, 256, 256), BF16),
            pltpu.VMEM((4, 256, 256), BF16),
            pltpu.VMEM((4, 256, 256), BF16),
            pltpu.VMEM((64, 512), BF16),
            pltpu.VMEM((256, 256), BF16),
            pltpu.VMEM((16, 64, 256), BF16),
            dma((5,)), dma, dma, dma((4,)), dma((4,)), dma, dma((4,)), dma, dma((4,)), dma, dma((4,)), dma, dma((4,)),
            dma((4,)), dma((4,)), dma, dma((4,)), dma, dma, dma, dma((4,)), dma, dma, dma, dma((2,)),
            dma, dma, dma, dma,
        ],
        compiler_params=pltpu.CompilerParams(
            collective_id=0, has_side_effects=True, vmem_limit_bytes=63 * 2**20
        ),
        name="attention_backward",
    )(queries, keys, values, outputs, gradient, jnp.transpose(sums, (0, 2, 1)), lengths)
    return pl.pallas_call(
        settle,
        out_shape=tuple(jax.ShapeDtypeStruct(m.shape, m.dtype) for m in made),
        in_specs=[hbm] * 3,
        out_specs=(hbm,) * 3,
        scratch_shapes=[pltpu.VMEM(m.shape, m.dtype) for m in made] + [dma((6,)), dma((6,))],
        compiler_params=pltpu.CompilerParams(vmem_limit_bytes=63 * 2**20),
        name="settle",
    )(*made)


def solution(mesh):
    in_specs = (
        P("ctx", "head", None),
        P("ctx", "head", None),
        P("ctx", "head", None),
        P("ctx", "head", None),
        P("ctx", "head", None),
        P("ctx", None, "head"),
        P(),
    )
    out_specs = (P("ctx", "head", None), P("ctx", "head", None), P("ctx", "head", None))
    return jax.shard_map(local, mesh=mesh, in_specs=in_specs, out_specs=out_specs, check_vma=False)
```

```python
import jax
import jax.numpy as jnp
from jax import lax
from jax.experimental import pallas as pl
from jax.experimental.pallas import tpu as pltpu
from jax.sharding import PartitionSpec as P

MESH = pl.DeviceIdType.MESH
F32 = jnp.float32
BF16 = jnp.bfloat16
SCALE = 128 ** (-0.5)
LOG2E = 1.4426950408889634
GROUPS = 16


def kernel(
    q_ref, k_ref, v_ref, o_ref, do_ref, lse_ref, len_ref,
    dq_ref, dk_ref, dv_ref,
    kin, ov, dov, kvs, kva, kvb, qb, dob, lset, lseb, dls, dlb, acc, dqt, dqs, dqr, pxs, pxr, rts, twin, via, ret,
    s_in, s_kv, s_kvn, r_kva, r_kvb, s_pa, r_pa, s_pb, r_pb, s_q, r_q, s_do, r_do,
    s_l, r_l, s_d, r_d, s_dq, r_dq, s_px, r_px, s_rt, s_rtp, r_rt, r_rtn, s_twin, r_twin, s_via, r_via,
):
    z = lax.axis_index("head")
    c = lax.axis_index("ctx")
    pair = c // 4
    own = c % 4
    xq = own // 2
    core = c % 2
    zb = z % 2
    zp = z // 2
    g = 2 * xq + zb
    first = pair == 0
    last = pair == GROUPS - 1
    before = pair == GROUPS // 2 - 1
    after = pair == GROUPS // 2
    bridge = before | after | first | last

    def zx(e):
        return (z, z + 1 - 2 * zb, (z + 2) % 4, 3 - z)[e]

    def xx(a):
        return xq if a == 0 else 1 - xq

    def kx(b):
        return core if b == 0 else 1 - core

    def at(off, a, b):
        return 4 * (pair + off) + 2 * xx(a) + kx(b)

    def remote(src, dst, ssem, rsem, dev):
        return pltpu.make_async_remote_copy(
            src_ref=src, dst_ref=dst, send_sem=ssem, recv_sem=rsem,
            device_id=dev, device_id_type=MESH,
        )

    def await_bytes(ref, sem):
        pltpu.make_async_copy(ref, ref, sem).wait()

    barrier = pltpu.get_barrier_semaphore()
    for a in range(2):
        for b in range(2):
            for e in range(4):
                if (a or b or e) and not (b and e == 3):
                    pl.semaphore_signal(barrier, inc=1, device_id=(zx(e), at(0, a, b)), device_id_type=MESH)

    @pl.when(jnp.logical_not(first))
    def _():
        for a in range(2):
            for e in range(4):
                pl.semaphore_signal(barrier, inc=1, device_id=(zx(e), at(-1, a, 0)), device_id_type=MESH)

    @pl.when(jnp.logical_not(last))
    def _():
        for a in range(2):
            for e in range(4):
                pl.semaphore_signal(barrier, inc=1, device_id=(zx(e), at(1, a, 0)), device_id_type=MESH)

    def greet(e, to):
        pl.semaphore_signal(barrier, inc=1, device_id=(zx(e), to), device_id_type=MESH)

    across = own + 4 * jnp.where(before, GROUPS - 1, jnp.where(last, GROUPS // 2 - 1, jnp.where(after, 0, GROUPS // 2)))
    aside = 2 * (1 - xq) + core + 4 * jnp.where(before, 0, jnp.where(first, GROUPS // 2 - 1, jnp.where(after, GROUPS - 1, GROUPS // 2)))

    @pl.when(bridge)
    def _():
        for e in range(4):
            greet(e, across)
        greet(0, aside)

    loads = [
        pltpu.make_async_copy(src, dst, s_in.at[n])
        for n, (src, dst) in enumerate(
            ((k_ref.at[0], kin.at[0]), (v_ref.at[0], kin.at[1]), (lse_ref.at[0], lset), (do_ref.at[0], dov), (o_ref.at[0], ov))
        )
    ]
    for load in loads:
        load.start()
    acc[...] = jnp.zeros_like(acc)

    place = lax.broadcasted_iota(jnp.int32, (8, 128), 1) + (pair * 1024 + zp * 128)

    def block_of(j):
        return 2 * ((xq + j // 2) % 2) + (core + j % 2) % 2

    def seek(d, carry):
        begin, found = carry
        found = tuple(jnp.where(place + 256 * block_of(n) >= begin, begin, f) for n, f in enumerate(found))
        return begin + len_ref[d], found

    _, opens = lax.fori_loop(0, 64, seek, (jnp.int32(0), tuple(jnp.zeros((8, 128), jnp.int32) for _ in range(4))))

    for load in loads[:2]:
        load.wait()
    for n in range(4):
        kvs[:, n * 256 : n * 256 + 128] = kin[0, :, n * 128 : (n + 1) * 128]
        kvs[:, n * 256 + 128 : (n + 1) * 256] = kin[1, :, n * 128 : (n + 1) * 128]

    pl.semaphore_wait(barrier, 13 + 8 * ((pair + GROUPS - 1) // GROUPS) + 8 * ((2 * GROUPS - 2 - pair) // GROUPS) + jnp.where(bridge, 5, 0))

    rows_own = pl.ds(pl.multiple_of(own * 256 + z * 64, 64), 64)

    def send_kv(off, a, e):
        there = 2 * xx(a) + zx(e) % 2
        src = kvs.at[:, pl.ds(pl.multiple_of(there * 256, 256), 256)]
        if off:
            remote(src, kva.at[rows_own], s_kvn, r_kva.at[own], (zx(e), at(1, a, 0))).start()
        elif a or e:
            remote(src, kvb.at[rows_own], s_kv, r_kvb.at[own], (zx(e), at(0, a, 0))).start()
        else:
            pltpu.make_async_copy(src, kvb.at[rows_own], r_kvb.at[own]).start()

    @pl.when(before)
    def _():
        for e in range(4):
            src = kvs.at[:, pl.ds(pl.multiple_of((2 * xq + zx(e) % 2) * 256, 256), 256)]
            remote(src, kva.at[rows_own], s_kvn, r_kva.at[own], (zx(e), at(1, 0, 0))).start()
        src = kvs.at[:, pl.ds(pl.multiple_of((1 - xq) * 512, 512), 512)]
        remote(src, twin, s_twin, r_twin, (z, aside)).start()

    for a, e in ((0, 0), (0, 2), (1, 0), (0, 3), (1, 2), (0, 1), (1, 3), (1, 1)):
        send_kv(0, a, e)

    @pl.when(jnp.logical_not(last | before))
    def _():
        for a, e in ((0, 2), (1, 2), (0, 3), (1, 3), (0, 0), (0, 1), (1, 0), (1, 1)):
            send_kv(1, a, e)

    for load in loads[2:]:
        load.wait()
    lanes = lax.broadcasted_iota(jnp.int32, (64, 128), 1)
    delta = jnp.zeros((64, 128), F32)
    for n in range(32):
        part = dov[:, n * 128 : (n + 1) * 128].astype(F32) * ov[:, n * 128 : (n + 1) * 128].astype(F32)
        delta = jnp.where(lanes == n, jnp.sum(part, axis=1, keepdims=True), delta)
    both = jnp.concatenate([delta, delta], axis=0).T
    for n in range(4):
        dls[n] = both[n * 8 : (n + 1) * 8]

    to_x = z // 2
    for e in (0, 2):
        half = zx(e) // 2
        for b in range(2):
            dev = (zx(e), 4 * pair + 2 * to_x + kx(b))
            slot = 2 * ((to_x + xq) % 2) + b
            src, dst = lset.at[:, pl.ds(pl.multiple_of(half * 128, 128), 128)], lseb.at[slot]
            if e == 0 and b == 0:
                @pl.when(to_x == xq)
                def _():
                    pltpu.make_async_copy(src, dst, r_l.at[slot]).start()

                @pl.when(to_x != xq)
                def _():
                    remote(src, dst, s_l.at[0], r_l.at[slot], dev).start()
            else:
                remote(src, dst, s_l.at[e + b], r_l.at[slot], dev).start()

    for a in range(2):
        for b in range(2):
            for e in range(2):
                src = dls.at[2 * xx(a) + zx(e) % 2]
                slot = 2 * a + b
                dst = dlb.at[pl.ds(pl.multiple_of(slot * 16 + zb * 8, 8), 8)]
                if a or b or e:
                    remote(src, dst, s_d, r_d.at[slot], (zx(e), at(0, a, b))).start()
                else:
                    pltpu.make_async_copy(src, dst, r_d.at[slot]).start()

    def send_queries(*which):
        for a, b, e in which:
            lane = (2 * xx(a) + zx(e) % 2) * 1024 + kx(b) * 512
            cols = pl.ds(pl.multiple_of(lane, 512), 512)
            for ref, buf, ss, rr in ((q_ref, qb, s_q, r_q), (do_ref, dob, s_do, r_do)):
                src = ref.at[0, :, cols]
                slot = 2 * a + b
                dst = buf.at[pl.ds(pl.multiple_of(slot * 128 + zb * 64, 64), 64)]
                if a or b or e:
                    remote(src, dst, ss, rr.at[slot], (zx(e), at(0, a, b))).start()
                else:
                    pltpu.make_async_copy(src, dst, rr.at[slot]).start()

    send_queries((0, 0, 0), (0, 1, 0), (1, 0, 0), (1, 1, 0), (0, 0, 1), (0, 1, 1))

    @pl.when(first)
    def _():
        await_bytes(twin, r_twin)
        theirs = 2 * (1 - xq) + core
        dst = kva.at[pl.ds(pl.multiple_of(theirs * 256 + z * 64, 64), 64)]
        for e in range(4):
            src = twin.at[:, pl.ds(pl.multiple_of(zx(e) % 2 * 256, 256), 256)]
            remote(src, dst, s_via, r_kva.at[theirs], (zx(e), across)).start()

    send_queries((1, 0, 1), (1, 1, 1))
    await_bytes(kvb.at[0 : 7 * 64], s_kv)

    for n in range(4):
        dqt[n] = jnp.zeros((128, 512), F32)
    def blk(b):
        return pl.ds(pl.multiple_of(b * 256, 256), 256)

    partner = (z, at(0, 0, 1))

    def hand_on(buf, sent, got, i):
        b = 2 * i + core
        remote(buf.at[blk(b)], buf.at[blk(b)], sent, got.at[b], partner).start()

    def own_blocks():
        for i in range(2):
            await_bytes(kvb.at[blk(2 * i + core)], r_kvb.at[2 * i + core])
            hand_on(kvb, s_pb, r_pb, i)
        for i in range(2):
            await_bytes(kvb.at[blk(2 * i + 1 - core)], r_pb.at[2 * i + 1 - core])

    def earlier_blocks():
        @pl.when(first)
        def _():
            kva[...] = jnp.zeros_like(kva)

        @pl.when(jnp.logical_not(first))
        def _():
            for i in range(2):
                await_bytes(kva.at[blk(2 * i + core)], r_kva.at[2 * i + core])
                hand_on(kva, s_pa, r_pa, i)
            for i in range(2):
                await_bytes(kva.at[blk(2 * i + 1 - core)], r_pa.at[2 * i + 1 - core])

    steps = lax.broadcasted_iota(jnp.int32, (256, 128), 0)
    low = lax.broadcasted_iota(jnp.int32, (8, 128), 1) < 64

    def work(j, buf, begin, end):
        bi = block_of(j)
        ahead = 4 if buf is kvb else 0
        lse_all = lseb[j]
        delta_all = jnp.where(low, dlb[j * 16 : j * 16 + 8], dlb[j * 16 + 8 : j * 16 + 16])
        lse_mine = jnp.where(core == 0, lse_all[0:4], lse_all[4:8])
        delta_mine = jnp.where(core == 0, delta_all[0:4], delta_all[4:8])
        lse_row = jnp.concatenate([lse_mine[n : n + 1] for n in range(4)], axis=1) * LOG2E
        delta_row = jnp.concatenate([delta_mine[n : n + 1] for n in range(4)], axis=1)
        where_open = opens[j][0:1]
        where_here = (place + 256 * bi)[0:1]
        qp = qb[j * 128 : (j + 1) * 128]
        dop = dob[j * 128 : (j + 1) * 128]
        qm = jnp.concatenate([qp[:, n * 128 : (n + 1) * 128] for n in range(4)], axis=0)
        dom = jnp.concatenate([dop[:, n * 128 : (n + 1) * 128] for n in range(4)], axis=0)

        def lag(b, _):
            rows = blk(b + ahead)
            key = buf[blk(b), 0:128]
            value = buf[blk(b), 128:256]
            base = (4 * pair - 4 + ahead + b) * 256
            allowed = (steps >= where_open - base) & (steps <= where_here - base)
            allowed = jnp.concatenate([allowed] * 4, axis=1)
            scores = lax.dot_general(key, qm, (((1,), (1,)), ((), ())), preferred_element_type=F32)
            weights = jnp.where(allowed, jnp.exp2(scores * (SCALE * LOG2E) - lse_row), 0.0)
            grads = lax.dot_general(value, dom, (((1,), (1,)), ((), ())), preferred_element_type=F32)
            shifted = (weights * (grads - delta_row) * SCALE).astype(BF16)
            acc[rows, 128:256] += jnp.dot(weights.astype(BF16), dom, preferred_element_type=F32)
            acc[rows, 0:128] += jnp.dot(shifted, qm, preferred_element_type=F32)
            dqt[j] += lax.dot_general(key, shifted, (((0,), (0,)), ((), ())), preferred_element_type=F32)
            return 0

        lax.fori_loop(begin, end, lag, 0)

    def arrived(j):
        await_bytes(lseb.at[j], r_l.at[j])
        await_bytes(dlb.at[j * 16 : (j + 1) * 16], r_d.at[j])
        await_bytes(qb.at[j * 128 : (j + 1) * 128], r_q.at[j])
        await_bytes(dob.at[j * 128 : (j + 1) * 128], r_do.at[j])

    def hand_back(j):
        for n in range(4):
            dqs[j * 128 : (j + 1) * 128, n * 128 : (n + 1) * 128] = dqt[j, :, n * 128 : (n + 1) * 128].T.astype(BF16)
        slot = 2 * g + core
        for e in (1, 0):
            src = dqs.at[pl.ds(pl.multiple_of(j * 128 + (zx(e) % 2) * 64, 64), 64)]
            dst = dqr.at[slot]
            if e or j:
                remote(src, dst, s_dq, r_dq, (zx(e), 4 * pair + block_of(j))).start()
            else:
                pltpu.make_async_copy(src, dst, r_dq).start()

    def to_partner(i):
        pxs[i] = acc[blk(2 * i + 1 - core)].astype(BF16)
        remote(pxs.at[i], pxr.at[i], s_px, r_px.at[i], partner).start()

    def from_partner(i):
        await_bytes(pxr.at[i], r_px.at[i])
        rts[i] = (acc[blk(2 * i + core)] + pxr[i].astype(F32)).astype(BF16)

    def send_back():
        for a in range(2):
            for e in range(4):
                src = rts.at[xx(a), pl.ds(pl.multiple_of(zx(e) * 64, 64), 64)]
                remote(src, ret.at[8 + xq * 4 + z], s_rtp, r_rtn.at[xq], (zx(e), at(-1, a, 0))).start()

    def send_own(i):
        for e in (2, 3, 1, 0):
            src = rts.at[i, pl.ds(pl.multiple_of(zx(e) * 64, 64), 64)]
            dst = ret.at[xq * 4 + z]
            far = remote(src, dst, s_rt, r_rt, (zx(e), 4 * pair + 2 * (i - 2) + core))
            if e:
                far.start()
            else:
                pl.when(xq != i - 2)(far.start)
                pl.when(xq == i - 2)(pltpu.make_async_copy(src, dst, r_rt).start)

    own_blocks()
    arrived(0)
    work(0, kvb, 0, block_of(0) + 1)
    earlier_blocks()
    work(0, kva, jnp.where(first, 4, block_of(0)), 4)
    hand_back(0)
    arrived(1)
    work(1, kvb, 0, block_of(1) + 1)
    work(1, kva, jnp.where(first, 4, block_of(1)), 4)
    hand_back(1)
    for j in range(2, 4):
        arrived(j)
        work(j, kva, jnp.where(first, 4, block_of(j)), 4)
    for i in range(2):
        to_partner(i)
    reach = tuple(jnp.minimum(block_of(j) + 1, 2) for j in (2, 3))
    work(2, kvb, 0, jnp.where(after, 0, reach[0]))
    for i in range(2):
        from_partner(i)

    @pl.when(jnp.logical_not(first | after))
    def _():
        send_back()

    @pl.when(after)
    def _():
        for e in range(4):
            part = pl.ds(pl.multiple_of(zx(e) * 64, 64), 64)
            remote(rts.at[xq, part], ret.at[8 + xq * 4 + z], s_rtp, r_rtn.at[xq], (zx(e), at(-1, 0, 0))).start()
        remote(rts.at[1 - xq], via, s_twin, r_via, (z, aside)).start()

    @pl.when(after)
    def _():
        work(2, kvb, 0, reach[0])

    work(3, kvb, 0, reach[1])
    to_partner(2)
    work(2, kvb, 2, block_of(2) + 1)
    hand_back(2)
    from_partner(2)
    send_own(2)
    work(3, kvb, 2, block_of(3) + 1)
    to_partner(3)
    hand_back(3)
    from_partner(3)
    send_own(3)

    @pl.when(last)
    def _():
        await_bytes(via, r_via)
        for e in range(4):
            src = via.at[pl.ds(pl.multiple_of(zx(e) * 64, 64), 64)]
            remote(src, ret.at[8 + (1 - xq) * 4 + z], s_via, r_rtn.at[1 - xq], (zx(e), across)).start()

    await_bytes(dqr, r_dq)
    for n in range(8):
        dq_ref[0, :, n * 512 : (n + 1) * 512] = dqr[n]
    await_bytes(ret.at[0:8], r_rt)

    @pl.when(last)
    def _():
        ret[8:16] = jnp.zeros((8, 64, 256), BF16)

    @pl.when(jnp.logical_not(last))
    def _():
        await_bytes(ret.at[8:12], r_rtn.at[0])
        await_bytes(ret.at[12:16], r_rtn.at[1])

    for n in range(4):
        total = jnp.zeros((64, 256), F32)
        for off in range(2):
            for p in range(2):
                total = total + ret[off * 8 + (n // 2) * 4 + 2 * p + n % 2].astype(F32)
        dk_ref[0, :, n * 128 : (n + 1) * 128] = total[:, 0:128].astype(BF16)
        dv_ref[0, :, n * 128 : (n + 1) * 128] = total[:, 128:256].astype(BF16)


    await_bytes(qb.at[0 : 7 * 64], s_q)
    await_bytes(dob.at[0 : 7 * 64], s_do)
    await_bytes(dqs.at[0 : 7 * 64], s_dq)
    await_bytes(pxs, s_px)
    await_bytes(ret.at[0:7], s_rt)
    await_bytes(dlb.at[0 : 7 * 8], s_d)
    for n in range(1, 4):
        await_bytes(lseb.at[0], s_l.at[n])

    @pl.when(to_x != xq)
    def _():
        await_bytes(lseb.at[0], s_l.at[0])

    @pl.when(before)
    def _():
        await_bytes(kvb.at[0:256], s_kvn)
        await_bytes(twin, s_twin)

    @pl.when(jnp.logical_not(last | before))
    def _():
        await_bytes(kvb.at[0:512], s_kvn)

    await_bytes(kvb.at[0:512], s_pb)

    @pl.when(jnp.logical_not(first))
    def _():
        await_bytes(kvb.at[0:512], s_pa)

    @pl.when(after)
    def _():
        await_bytes(ret.at[0:4], s_rtp)
        await_bytes(via, s_twin)

    @pl.when(jnp.logical_not(first | after))
    def _():
        await_bytes(ret.at[0:8], s_rtp)

    @pl.when(first | last)
    def _():
        await_bytes(via, s_via)


def settle(dq_in, dk_in, dv_in, dq_ref, dk_ref, dv_ref, dq_held, dk_held, dv_held, s_in, s_out):
    moves = [(dk_in, dk_held, dk_ref), (dv_in, dv_held, dv_ref)]
    for n in range(4):
        rows = slice(n * 16, (n + 1) * 16)
        moves.append((dq_in.at[:, rows], dq_held.at[:, rows], dq_ref.at[:, rows]))
    came = [pltpu.make_async_copy(src, held, s_in.at[n]) for n, (src, held, _) in enumerate(moves)]
    goes = [pltpu.make_async_copy(held, dst, s_out.at[n]) for n, (_, held, dst) in enumerate(moves)]
    for copy in came:
        copy.start()
    for one, other in zip(came, goes):
        one.wait()
        other.start()
    for copy in goes:
        copy.wait()


def local(queries, keys, values, outputs, gradient, sums, lengths):
    vmem = pl.BlockSpec(memory_space=pltpu.VMEM)
    hbm = pl.BlockSpec(memory_space=pltpu.HBM)
    dma = pltpu.SemaphoreType.DMA
    made = pl.pallas_call(
        kernel,
        out_shape=(
            jax.ShapeDtypeStruct((1, 64, 4096), BF16),
            jax.ShapeDtypeStruct((1, 64, 512), BF16),
            jax.ShapeDtypeStruct((1, 64, 512), BF16),
        ),
        in_specs=[hbm] * 6 + [pl.BlockSpec(memory_space=pltpu.SMEM)],
        out_specs=(vmem, vmem, vmem),
        scratch_shapes=[
            pltpu.VMEM((2, 64, 512), BF16),
            pltpu.VMEM((64, 4096), BF16),
            pltpu.VMEM((64, 4096), BF16),
            pltpu.VMEM((64, 1024), BF16),
            pltpu.VMEM((1024, 256), BF16),
            pltpu.VMEM((1024, 256), BF16),
            pltpu.VMEM((512, 512), BF16),
            pltpu.VMEM((512, 512), BF16),
            pltpu.VMEM((8, 256), F32),
            pltpu.VMEM((4, 8, 128), F32),
            pltpu.VMEM((4, 8, 128), F32),
            pltpu.VMEM((64, 128), F32),
            pltpu.VMEM((2048, 256), F32),
            pltpu.VMEM((4, 128, 512), F32),
            pltpu.VMEM((512, 512), BF16),
            pltpu.VMEM((8, 64, 512), BF16),
            pltpu.VMEM((4, 256, 256), BF16),
            pltpu.VMEM((4, 256, 256), BF16),
            pltpu.VMEM((4, 256, 256), BF16),
            pltpu.VMEM((64, 512), BF16),
            pltpu.VMEM((256, 256), BF16),
            pltpu.VMEM((16, 64, 256), BF16),
            dma((5,)), dma, dma, dma((4,)), dma((4,)), dma, dma((4,)), dma, dma((4,)), dma, dma((4,)), dma, dma((4,)),
            dma((4,)), dma((4,)), dma, dma((4,)), dma, dma, dma, dma((4,)), dma, dma, dma, dma((2,)),
            dma, dma, dma, dma,
        ],
        compiler_params=pltpu.CompilerParams(
            collective_id=0, has_side_effects=True, vmem_limit_bytes=63 * 2**20
        ),
        name="attention_backward",
    )(queries, keys, values, outputs, gradient, jnp.transpose(sums, (0, 2, 1)), lengths)
    return pl.pallas_call(
        settle,
        out_shape=tuple(jax.ShapeDtypeStruct(m.shape, m.dtype) for m in made),
        in_specs=[hbm] * 3,
        out_specs=(hbm,) * 3,
        scratch_shapes=[pltpu.VMEM(m.shape, m.dtype) for m in made] + [dma((6,)), dma((6,))],
        compiler_params=pltpu.CompilerParams(vmem_limit_bytes=63 * 2**20),
        name="settle",
    )(*made)


def solution(mesh):
    in_specs = (
        P("ctx", "head", None),
        P("ctx", "head", None),
        P("ctx", "head", None),
        P("ctx", "head", None),
        P("ctx", "head", None),
        P("ctx", None, "head"),
        P(),
    )
    out_specs = (P("ctx", "head", None), P("ctx", "head", None), P("ctx", "head", None))
    return jax.shard_map(local, mesh=mesh, in_specs=in_specs, out_specs=out_specs, check_vma=False)
```

```python
import jax
import jax.numpy as jnp
from jax import lax
from jax.experimental import pallas as pl
from jax.experimental.pallas import tpu as pltpu
from jax.sharding import PartitionSpec as P

MESH = pl.DeviceIdType.MESH
F32 = jnp.float32
BF16 = jnp.bfloat16
SCALE = 128 ** (-0.5)
LOG2E = 1.4426950408889634
GROUPS = 16


def kernel(
    q_ref, k_ref, v_ref, o_ref, do_ref, lse_ref, len_ref,
    dq_ref, dk_ref, dv_ref,
    kin, ov, dov, kvs, kva, kvb, qb, dob, lset, lseb, dls, dlb, acc, dqt, dqs, dqr, pxs, pxr, rts, twin, via, ret,
    s_in, s_kv, s_kvn, r_kva, r_kvb, s_pa, r_pa, s_pb, r_pb, s_q, r_q, s_do, r_do,
    s_l, r_l, s_d, r_d, s_dq, r_dq, s_px, r_px, s_rt, s_rtp, r_rt, r_rtn, s_twin, r_twin, s_via, r_via,
):
    z = lax.axis_index("head")
    c = lax.axis_index("ctx")
    pair = c // 4
    own = c % 4
    xq = own // 2
    core = c % 2
    zb = z % 2
    zp = z // 2
    g = 2 * xq + zb
    first = pair == 0
    last = pair == GROUPS - 1
    before = pair == GROUPS // 2 - 1
    after = pair == GROUPS // 2
    bridge = before | after | first | last

    def zx(e):
        return (z, z + 1 - 2 * zb, (z + 2) % 4, 3 - z)[e]

    def xx(a):
        return xq if a == 0 else 1 - xq

    def kx(b):
        return core if b == 0 else 1 - core

    def at(off, a, b):
        return 4 * (pair + off) + 2 * xx(a) + kx(b)

    def remote(src, dst, ssem, rsem, dev):
        return pltpu.make_async_remote_copy(
            src_ref=src, dst_ref=dst, send_sem=ssem, recv_sem=rsem,
            device_id=dev, device_id_type=MESH,
        )

    def await_bytes(ref, sem):
        pltpu.make_async_copy(ref, ref, sem).wait()

    barrier = pltpu.get_barrier_semaphore()
    for a in range(2):
        for b in range(2):
            for e in range(4):
                if (a or b or e) and not (b and e == 3):
                    pl.semaphore_signal(barrier, inc=1, device_id=(zx(e), at(0, a, b)), device_id_type=MESH)

    @pl.when(jnp.logical_not(first))
    def _():
        for a in range(2):
            for e in range(4):
                pl.semaphore_signal(barrier, inc=1, device_id=(zx(e), at(-1, a, 0)), device_id_type=MESH)

    @pl.when(jnp.logical_not(last))
    def _():
        for a in range(2):
            for e in range(4):
                pl.semaphore_signal(barrier, inc=1, device_id=(zx(e), at(1, a, 0)), device_id_type=MESH)

    def greet(e, to):
        pl.semaphore_signal(barrier, inc=1, device_id=(zx(e), to), device_id_type=MESH)

    across = own + 4 * jnp.where(before, GROUPS - 1, jnp.where(last, GROUPS // 2 - 1, jnp.where(after, 0, GROUPS // 2)))
    aside = 2 * (1 - xq) + core + 4 * jnp.where(before, 0, jnp.where(first, GROUPS // 2 - 1, jnp.where(after, GROUPS - 1, GROUPS // 2)))

    @pl.when(bridge)
    def _():
        for e in range(4):
            greet(e, across)
        greet(0, aside)

    loads = [
        pltpu.make_async_copy(src, dst, s_in.at[n])
        for n, (src, dst) in enumerate(
            ((k_ref.at[0], kin.at[0]), (v_ref.at[0], kin.at[1]), (lse_ref.at[0], lset), (do_ref.at[0], dov), (o_ref.at[0], ov))
        )
    ]
    for load in loads:
        load.start()
    acc[...] = jnp.zeros_like(acc)

    place = lax.broadcasted_iota(jnp.int32, (8, 128), 1) + (pair * 1024 + zp * 128)

    def block_of(j):
        return 2 * ((xq + j // 2) % 2) + (core + j % 2) % 2

    def seek(d, carry):
        begin, found = carry
        found = tuple(jnp.where(place + 256 * block_of(n) >= begin, begin, f) for n, f in enumerate(found))
        return begin + len_ref[d], found

    _, opens = lax.fori_loop(0, 64, seek, (jnp.int32(0), tuple(jnp.zeros((8, 128), jnp.int32) for _ in range(4))))

    for load in loads[:2]:
        load.wait()
    for n in range(4):
        kvs[:, n * 256 : n * 256 + 128] = kin[0, :, n * 128 : (n + 1) * 128]
        kvs[:, n * 256 + 128 : (n + 1) * 256] = kin[1, :, n * 128 : (n + 1) * 128]

    pl.semaphore_wait(barrier, 13 + 8 * ((pair + GROUPS - 1) // GROUPS) + 8 * ((2 * GROUPS - 2 - pair) // GROUPS) + jnp.where(bridge, 5, 0))

    rows_own = pl.ds(pl.multiple_of(own * 256 + z * 64, 64), 64)

    def send_kv(off, a, e):
        there = 2 * xx(a) + zx(e) % 2
        src = kvs.at[:, pl.ds(pl.multiple_of(there * 256, 256), 256)]
        if off:
            remote(src, kva.at[rows_own], s_kvn, r_kva.at[own], (zx(e), at(1, a, 0))).start()
        elif a or e:
            remote(src, kvb.at[rows_own], s_kv, r_kvb.at[own], (zx(e), at(0, a, 0))).start()
        else:
            pltpu.make_async_copy(src, kvb.at[rows_own], r_kvb.at[own]).start()

    @pl.when(before)
    def _():
        for e in range(4):
            src = kvs.at[:, pl.ds(pl.multiple_of((2 * xq + zx(e) % 2) * 256, 256), 256)]
            remote(src, kva.at[rows_own], s_kvn, r_kva.at[own], (zx(e), at(1, 0, 0))).start()
        src = kvs.at[:, pl.ds(pl.multiple_of((1 - xq) * 512, 512), 512)]
        remote(src, twin, s_twin, r_twin, (z, aside)).start()

    for a, e in ((0, 0), (0, 2), (1, 0), (0, 3), (1, 2), (0, 1), (1, 3), (1, 1)):
        send_kv(0, a, e)

    @pl.when(jnp.logical_not(last | before))
    def _():
        for a, e in ((0, 2), (1, 2), (0, 3), (1, 3), (0, 0), (0, 1), (1, 0), (1, 1)):
            send_kv(1, a, e)

    for load in loads[2:]:
        load.wait()
    lanes = lax.broadcasted_iota(jnp.int32, (64, 128), 1)
    delta = jnp.zeros((64, 128), F32)
    for n in range(32):
        part = dov[:, n * 128 : (n + 1) * 128].astype(F32) * ov[:, n * 128 : (n + 1) * 128].astype(F32)
        delta = jnp.where(lanes == n, jnp.sum(part, axis=1, keepdims=True), delta)
    both = jnp.concatenate([delta, delta], axis=0).T
    for n in range(4):
        dls[n] = both[n * 8 : (n + 1) * 8]

    to_x = z // 2
    for e in (0, 2):
        half = zx(e) // 2
        for b in range(2):
            dev = (zx(e), 4 * pair + 2 * to_x + kx(b))
            slot = 2 * ((to_x + xq) % 2) + b
            src, dst = lset.at[:, pl.ds(pl.multiple_of(half * 128, 128), 128)], lseb.at[slot]
            if e == 0 and b == 0:
                @pl.when(to_x == xq)
                def _():
                    pltpu.make_async_copy(src, dst, r_l.at[slot]).start()

                @pl.when(to_x != xq)
                def _():
                    remote(src, dst, s_l.at[0], r_l.at[slot], dev).start()
            else:
                remote(src, dst, s_l.at[e + b], r_l.at[slot], dev).start()

    for a in range(2):
        for b in range(2):
            for e in range(2):
                src = dls.at[2 * xx(a) + zx(e) % 2]
                slot = 2 * a + b
                dst = dlb.at[pl.ds(pl.multiple_of(slot * 16 + zb * 8, 8), 8)]
                if a or b or e:
                    remote(src, dst, s_d, r_d.at[slot], (zx(e), at(0, a, b))).start()
                else:
                    pltpu.make_async_copy(src, dst, r_d.at[slot]).start()

    def send_queries(*which):
        for a, b, e in which:
            lane = (2 * xx(a) + zx(e) % 2) * 1024 + kx(b) * 512
            cols = pl.ds(pl.multiple_of(lane, 512), 512)
            for ref, buf, ss, rr in ((q_ref, qb, s_q, r_q), (do_ref, dob, s_do, r_do)):
                src = ref.at[0, :, cols]
                slot = 2 * a + b
                dst = buf.at[pl.ds(pl.multiple_of(slot * 128 + zb * 64, 64), 64)]
                if a or b or e:
                    remote(src, dst, ss, rr.at[slot], (zx(e), at(0, a, b))).start()
                else:
                    pltpu.make_async_copy(src, dst, rr.at[slot]).start()

    send_queries((0, 0, 0), (0, 1, 0), (1, 0, 0), (1, 1, 0), (0, 0, 1), (0, 1, 1))

    @pl.when(first)
    def _():
        await_bytes(twin, r_twin)
        theirs = 2 * (1 - xq) + core
        dst = kva.at[pl.ds(pl.multiple_of(theirs * 256 + z * 64, 64), 64)]
        for e in range(4):
            src = twin.at[:, pl.ds(pl.multiple_of(zx(e) % 2 * 256, 256), 256)]
            remote(src, dst, s_via, r_kva.at[theirs], (zx(e), across)).start()

    send_queries((1, 0, 1), (1, 1, 1))
    await_bytes(kvb.at[0 : 7 * 64], s_kv)

    for n in range(4):
        dqt[n] = jnp.zeros((128, 512), F32)
    def blk(b):
        return pl.ds(pl.multiple_of(b * 256, 256), 256)

    partner = (z, at(0, 0, 1))

    def hand_on(buf, sent, got, i):
        b = 2 * i + core
        remote(buf.at[blk(b)], buf.at[blk(b)], sent, got.at[b], partner).start()

    def own_blocks():
        for i in range(2):
            await_bytes(kvb.at[blk(2 * i + core)], r_kvb.at[2 * i + core])
            hand_on(kvb, s_pb, r_pb, i)
        for i in range(2):
            await_bytes(kvb.at[blk(2 * i + 1 - core)], r_pb.at[2 * i + 1 - core])

    def earlier_blocks():
        @pl.when(first)
        def _():
            kva[...] = jnp.zeros_like(kva)

        @pl.when(jnp.logical_not(first))
        def _():
            for i in range(2):
                await_bytes(kva.at[blk(2 * i + core)], r_kva.at[2 * i + core])
                hand_on(kva, s_pa, r_pa, i)
            for i in range(2):
                await_bytes(kva.at[blk(2 * i + 1 - core)], r_pa.at[2 * i + 1 - core])

    steps = lax.broadcasted_iota(jnp.int32, (256, 128), 0)
    low = lax.broadcasted_iota(jnp.int32, (8, 128), 1) < 64

    def work(j, buf, begin, end):
        bi = block_of(j)
        ahead = 4 if buf is kvb else 0
        lse_all = lseb[j]
        delta_all = jnp.where(low, dlb[j * 16 : j * 16 + 8], dlb[j * 16 + 8 : j * 16 + 16])
        lse_mine = jnp.where(core == 0, lse_all[0:4], lse_all[4:8])
        delta_mine = jnp.where(core == 0, delta_all[0:4], delta_all[4:8])
        lse_row = jnp.concatenate([lse_mine[n : n + 1] for n in range(4)], axis=1) * LOG2E
        delta_row = jnp.concatenate([delta_mine[n : n + 1] for n in range(4)], axis=1)
        where_open = opens[j][0:1]
        where_here = (place + 256 * bi)[0:1]
        qp = qb[j * 128 : (j + 1) * 128]
        dop = dob[j * 128 : (j + 1) * 128]
        qm = jnp.concatenate([qp[:, n * 128 : (n + 1) * 128] for n in range(4)], axis=0)
        dom = jnp.concatenate([dop[:, n * 128 : (n + 1) * 128] for n in range(4)], axis=0)

        def lag(b, _):
            rows = blk(b + ahead)
            key = buf[blk(b), 0:128]
            value = buf[blk(b), 128:256]
            base = (4 * pair - 4 + ahead + b) * 256
            allowed = (steps >= where_open - base) & (steps <= where_here - base)
            allowed = jnp.concatenate([allowed] * 4, axis=1)
            scores = lax.dot_general(key, qm, (((1,), (1,)), ((), ())), preferred_element_type=F32)
            weights = jnp.where(allowed, jnp.exp2(scores * (SCALE * LOG2E) - lse_row), 0.0)
            grads = lax.dot_general(value, dom, (((1,), (1,)), ((), ())), preferred_element_type=F32)
            shifted = (weights * (grads - delta_row) * SCALE).astype(BF16)
            acc[rows, 128:256] += jnp.dot(weights.astype(BF16), dom, preferred_element_type=F32)
            acc[rows, 0:128] += jnp.dot(shifted, qm, preferred_element_type=F32)
            dqt[j] += lax.dot_general(key, shifted, (((0,), (0,)), ((), ())), preferred_element_type=F32)
            return 0

        lax.fori_loop(begin, end, lag, 0)

    def arrived(j):
        await_bytes(lseb.at[j], r_l.at[j])
        await_bytes(dlb.at[j * 16 : (j + 1) * 16], r_d.at[j])
        await_bytes(qb.at[j * 128 : (j + 1) * 128], r_q.at[j])
        await_bytes(dob.at[j * 128 : (j + 1) * 128], r_do.at[j])

    def hand_back(j):
        for n in range(4):
            dqs[j * 128 : (j + 1) * 128, n * 128 : (n + 1) * 128] = dqt[j, :, n * 128 : (n + 1) * 128].T.astype(BF16)
        slot = 2 * g + core
        for e in (1, 0):
            src = dqs.at[pl.ds(pl.multiple_of(j * 128 + (zx(e) % 2) * 64, 64), 64)]
            dst = dqr.at[slot]
            if e or j:
                remote(src, dst, s_dq, r_dq, (zx(e), 4 * pair + block_of(j))).start()
            else:
                pltpu.make_async_copy(src, dst, r_dq).start()

    def to_partner(i):
        pxs[i] = acc[blk(2 * i + 1 - core)].astype(BF16)
        remote(pxs.at[i], pxr.at[i], s_px, r_px.at[i], partner).start()

    def from_partner(i):
        await_bytes(pxr.at[i], r_px.at[i])
        rts[i] = (acc[blk(2 * i + core)] + pxr[i].astype(F32)).astype(BF16)

    def send_back():
        for a in range(2):
            for e in range(4):
                src = rts.at[xx(a), pl.ds(pl.multiple_of(zx(e) * 64, 64), 64)]
                remote(src, ret.at[8 + xq * 4 + z], s_rtp, r_rtn.at[xq], (zx(e), at(-1, a, 0))).start()

    def send_own(i):
        for e in (2, 3, 1, 0):
            src = rts.at[i, pl.ds(pl.multiple_of(zx(e) * 64, 64), 64)]
            dst = ret.at[xq * 4 + z]
            far = remote(src, dst, s_rt, r_rt, (zx(e), 4 * pair + 2 * (i - 2) + core))
            if e:
                far.start()
            else:
                pl.when(xq != i - 2)(far.start)
                pl.when(xq == i - 2)(pltpu.make_async_copy(src, dst, r_rt).start)

    own_blocks()
    arrived(0)
    work(0, kvb, 0, block_of(0) + 1)
    earlier_blocks()
    work(0, kva, jnp.where(first, 4, block_of(0)), 4)
    hand_back(0)
    arrived(1)
    work(1, kvb, 0, block_of(1) + 1)
    work(1, kva, jnp.where(first, 4, block_of(1)), 4)
    hand_back(1)
    for j in range(2, 4):
        arrived(j)
        work(j, kva, jnp.where(first, 4, block_of(j)), 4)
    for i in range(2):
        to_partner(i)
    reach = tuple(jnp.minimum(block_of(j) + 1, 2) for j in (2, 3))
    work(2, kvb, 0, jnp.where(after, 0, reach[0]))
    for i in range(2):
        from_partner(i)

    @pl.when(jnp.logical_not(first | after))
    def _():
        send_back()

    @pl.when(after)
    def _():
        for e in range(4):
            part = pl.ds(pl.multiple_of(zx(e) * 64, 64), 64)
            remote(rts.at[xq, part], ret.at[8 + xq * 4 + z], s_rtp, r_rtn.at[xq], (zx(e), at(-1, 0, 0))).start()
        remote(rts.at[1 - xq], via, s_twin, r_via, (z, aside)).start()

    @pl.when(after)
    def _():
        work(2, kvb, 0, reach[0])

    work(3, kvb, 0, reach[1])
    to_partner(2)
    work(2, kvb, 2, block_of(2) + 1)
    hand_back(2)
    from_partner(2)
    send_own(2)
    work(3, kvb, 2, block_of(3) + 1)
    to_partner(3)
    hand_back(3)
    from_partner(3)
    send_own(3)

    @pl.when(last)
    def _():
        await_bytes(via, r_via)
        for e in range(4):
            src = via.at[pl.ds(pl.multiple_of(zx(e) * 64, 64), 64)]
            remote(src, ret.at[8 + (1 - xq) * 4 + z], s_via, r_rtn.at[1 - xq], (zx(e), across)).start()

    await_bytes(dqr, r_dq)
    for n in range(8):
        dq_ref[0, :, n * 512 : (n + 1) * 512] = dqr[n]
    await_bytes(ret.at[0:8], r_rt)

    @pl.when(last)
    def _():
        ret[8:16] = jnp.zeros((8, 64, 256), BF16)

    @pl.when(jnp.logical_not(last))
    def _():
        await_bytes(ret.at[8:12], r_rtn.at[0])
        await_bytes(ret.at[12:16], r_rtn.at[1])

    for n in range(4):
        total = jnp.zeros((64, 256), F32)
        for off in range(2):
            for p in range(2):
                total = total + ret[off * 8 + (n // 2) * 4 + 2 * p + n % 2].astype(F32)
        dk_ref[0, :, n * 128 : (n + 1) * 128] = total[:, 0:128].astype(BF16)
        dv_ref[0, :, n * 128 : (n + 1) * 128] = total[:, 128:256].astype(BF16)


    await_bytes(qb.at[0 : 7 * 64], s_q)
    await_bytes(dob.at[0 : 7 * 64], s_do)
    await_bytes(dqs.at[0 : 7 * 64], s_dq)
    await_bytes(pxs, s_px)
    await_bytes(ret.at[0:7], s_rt)
    await_bytes(dlb.at[0 : 7 * 8], s_d)
    for n in range(1, 4):
        await_bytes(lseb.at[0], s_l.at[n])

    @pl.when(to_x != xq)
    def _():
        await_bytes(lseb.at[0], s_l.at[0])

    @pl.when(before)
    def _():
        await_bytes(kvb.at[0:256], s_kvn)
        await_bytes(twin, s_twin)

    @pl.when(jnp.logical_not(last | before))
    def _():
        await_bytes(kvb.at[0:512], s_kvn)

    await_bytes(kvb.at[0:512], s_pb)

    @pl.when(jnp.logical_not(first))
    def _():
        await_bytes(kvb.at[0:512], s_pa)

    @pl.when(after)
    def _():
        await_bytes(ret.at[0:4], s_rtp)
        await_bytes(via, s_twin)

    @pl.when(jnp.logical_not(first | after))
    def _():
        await_bytes(ret.at[0:8], s_rtp)

    @pl.when(first | last)
    def _():
        await_bytes(via, s_via)


def settle(dq_in, dk_in, dv_in, dq_ref, dk_ref, dv_ref, dq_held, dk_held, dv_held, s_in, s_out):
    moves = []
    for n in range(2):
        rows = slice(n * 32, (n + 1) * 32)
        moves.append((dq_in.at[:, rows], dq_held.at[:, rows], dq_ref.at[:, rows]))
    moves += [(dk_in, dk_held, dk_ref), (dv_in, dv_held, dv_ref)]
    came = [pltpu.make_async_copy(src, held, s_in.at[n]) for n, (src, held, _) in enumerate(moves)]
    goes = [pltpu.make_async_copy(held, dst, s_out.at[n]) for n, (_, held, dst) in enumerate(moves)]
    for copy in came:
        copy.start()
    for one, other in zip(came, goes):
        one.wait()
        other.start()
    for copy in goes:
        copy.wait()


def local(queries, keys, values, outputs, gradient, sums, lengths):
    vmem = pl.BlockSpec(memory_space=pltpu.VMEM)
    hbm = pl.BlockSpec(memory_space=pltpu.HBM)
    dma = pltpu.SemaphoreType.DMA
    made = pl.pallas_call(
        kernel,
        out_shape=(
            jax.ShapeDtypeStruct((1, 64, 4096), BF16),
            jax.ShapeDtypeStruct((1, 64, 512), BF16),
            jax.ShapeDtypeStruct((1, 64, 512), BF16),
        ),
        in_specs=[hbm] * 6 + [pl.BlockSpec(memory_space=pltpu.SMEM)],
        out_specs=(vmem, vmem, vmem),
        scratch_shapes=[
            pltpu.VMEM((2, 64, 512), BF16),
            pltpu.VMEM((64, 4096), BF16),
            pltpu.VMEM((64, 4096), BF16),
            pltpu.VMEM((64, 1024), BF16),
            pltpu.VMEM((1024, 256), BF16),
            pltpu.VMEM((1024, 256), BF16),
            pltpu.VMEM((512, 512), BF16),
            pltpu.VMEM((512, 512), BF16),
            pltpu.VMEM((8, 256), F32),
            pltpu.VMEM((4, 8, 128), F32),
            pltpu.VMEM((4, 8, 128), F32),
            pltpu.VMEM((64, 128), F32),
            pltpu.VMEM((2048, 256), F32),
            pltpu.VMEM((4, 128, 512), F32),
            pltpu.VMEM((512, 512), BF16),
            pltpu.VMEM((8, 64, 512), BF16),
            pltpu.VMEM((4, 256, 256), BF16),
            pltpu.VMEM((4, 256, 256), BF16),
            pltpu.VMEM((4, 256, 256), BF16),
            pltpu.VMEM((64, 512), BF16),
            pltpu.VMEM((256, 256), BF16),
            pltpu.VMEM((16, 64, 256), BF16),
            dma((5,)), dma, dma, dma((4,)), dma((4,)), dma, dma((4,)), dma, dma((4,)), dma, dma((4,)), dma, dma((4,)),
            dma((4,)), dma((4,)), dma, dma((4,)), dma, dma, dma, dma((4,)), dma, dma, dma, dma((2,)),
            dma, dma, dma, dma,
        ],
        compiler_params=pltpu.CompilerParams(
            collective_id=0, has_side_effects=True, vmem_limit_bytes=63 * 2**20
        ),
        name="attention_backward",
    )(queries, keys, values, outputs, gradient, jnp.transpose(sums, (0, 2, 1)), lengths)
    return pl.pallas_call(
        settle,
        out_shape=tuple(jax.ShapeDtypeStruct(m.shape, m.dtype) for m in made),
        in_specs=[hbm] * 3,
        out_specs=(hbm,) * 3,
        scratch_shapes=[pltpu.VMEM(m.shape, m.dtype) for m in made] + [dma((4,)), dma((4,))],
        compiler_params=pltpu.CompilerParams(vmem_limit_bytes=63 * 2**20),
        name="settle",
    )(*made)


def solution(mesh):
    in_specs = (
        P("ctx", "head", None),
        P("ctx", "head", None),
        P("ctx", "head", None),
        P("ctx", "head", None),
        P("ctx", "head", None),
        P("ctx", None, "head"),
        P(),
    )
    out_specs = (P("ctx", "head", None), P("ctx", "head", None), P("ctx", "head", None))
    return jax.shard_map(local, mesh=mesh, in_specs=in_specs, out_specs=out_specs, check_vma=False)
```
